256 devices in a mesh: flow: 16 (over z, x_hi), grad: 16 (over y, x_lo, core).
Axes of the slice: x: 4 (x_hi: 2, x_lo: 2; x = x_hi * 2 + x_lo), y: 4, z: 8, core: 2. Of those that a mesh axis runs over, the one named last changes fastest.
Arguments:
- populations: float32 [19, 128, 128, 128], P(None, 'flow', 'grad'), may hold values from 0.008 to 1.01, as said below
- le_offset: int32 [1], replicated, may hold values from 0 to 127
- sphere_velocity: float32 [3, 16, 16, 64], P(None, 'flow', 'grad'), may hold values from -0.4 to 0.4
- link_cell: int32 [16, 16, 16384], P('flow', 'grad'), may hold values from 0 to 8191, as said below
- link_dir: int32 [16, 16, 16384], P('flow', 'grad'), may hold values from 1 to 18, as said below
- link_sphere: int32 [16, 16, 16384], P('flow', 'grad'), may hold values from 0 to 575
- link_count: int32 [16, 16], P('flow', 'grad'), may hold values from 4096 to 16384, as said below
- pair_first: int32 [16, 16, 256], P('flow', 'grad'), may hold values from 0 to 63
- pair_second: int32 [16, 16, 256], P('flow', 'grad'), may hold values from 0 to 575
- pair_count: int32 [16, 16], P('flow', 'grad'), may hold values from 64 to 256, as said below
- pair_gap: float32 [16, 16, 256], P('flow', 'grad'), may hold values from 0.02 to 1
- pair_normal: float32 [3, 16, 16, 256], P(None, 'flow', 'grad'), may hold values from -1 to 1
Outputs:
- populations_next: float32 [19, 128, 128, 128], P(None, 'flow', 'grad')
- sphere_force: float32 [3, 16, 16, 64], P(None, 'flow', 'grad')
- velocity_next: float32 [3, 16, 16, 64], P(None, 'flow', 'grad')
The draws below stay inside these ranges and needn't reach their ends.
Inputs may be any that keep to these rules, and one draw needn't show every extreme that they name: `populations`: each population lies between 0.3 and 3 times its direction's lattice weight. `link_cell`: local cell numbers (x_local * 8 + y_local) * 128 + z; within one tile no two link slots name the same cell and direction, and a cell may carry several links. `link_dir`: within one tile no two link slots name the same cell and direction. Live links of a tile are its first link_count slots; in every draw some tile has all 16384 slots live. Live pairs of a tile are its first pair_count slots; in every draw some tile has all 256 slots live.
All inputs are finite; a program needn't handle non-finite values.
Results may differ from the reference program's by a relative error of at most 0.0003.
Values sent between devices are 32-bit elements; how exact they have to be, the bound alone decides.
A program may use at most 64 MiB of HBM per device.

```python
import math
import jax
import jax.numpy as jnp
from jax import lax

CX = 8
CY = 8
NZ = 128
LINKS_DEV = 16384
SPH_DEV = 64
PAIRS_DEV = 256
NX = 128
NY = 128
N_FLOW = 16
N_GRAD = 16


LATTICE_WEIGHTS = [1.0 / 3.0] + [1.0 / 18.0] * 6 + [1.0 / 36.0] * 12


def draw_populations(key, part):
    shape = (19, NX, NY, NZ)
    weights = jnp.asarray(LATTICE_WEIGHTS, jnp.float32).reshape(19, 1, 1, 1)
    factor = jnp.exp(jax.random.uniform(key, shape, jnp.float32, math.log(0.3), math.log(3.0)))
    return weights * factor


def link_codes(key):
    tiles = N_FLOW * N_GRAD
    keys = jax.random.split(jax.random.fold_in(key, 11), tiles)

    def one_tile(single):
        return jax.random.permutation(single, 18 * CX * CY * NZ)[:LINKS_DEV]
    picked_codes = lax.map(one_tile, keys)
    return picked_codes.reshape(N_FLOW, N_GRAD, LINKS_DEV).astype(jnp.int32)


def draw_link_cell(key, part):
    return link_codes(key) // 18


def draw_link_dir(key, part):
    return link_codes(key) % 18 + 1


def full_counts(key, largest):
    tiles = N_FLOW * N_GRAD
    counts = jax.random.randint(key, (tiles,), largest // 4, largest + 1, jnp.int32)
    chosen = jax.random.randint(jax.random.fold_in(key, 7), (), 0, tiles)
    return counts.at[chosen].set(largest).reshape(N_FLOW, N_GRAD)


def draw_link_count(key, part):
    return full_counts(jax.random.fold_in(key, 21), LINKS_DEV)


def draw_pair_count(key, part):
    return full_counts(jax.random.fold_in(key, 31), PAIRS_DEV)


def draw_pair_normal(key, part):
    shape = (N_FLOW, N_GRAD, PAIRS_DEV)
    polar = jnp.arccos(jax.random.uniform(jax.random.fold_in(key, 41), shape, jnp.float32, -1.0, 1.0))
    azimuth = jax.random.uniform(jax.random.fold_in(key, 42), shape, jnp.float32, -math.pi, math.pi)
    return jnp.stack([jnp.sin(polar) * jnp.cos(azimuth), jnp.sin(polar) * jnp.sin(azimuth), jnp.cos(polar)])


def plant(entries, own_key, least, high):
    dims = entries.shape
    place = [jax.random.randint(jax.random.fold_in(own_key, axis), (), 0, dims[axis]) for axis in range(len(dims))]
    entries = entries.at[tuple(place)].set(least)
    longest = dims.index(max(dims))
    place[longest] = (place[longest] + 1) % dims[longest]
    return entries.at[tuple(place)].set(high)


def shard_levels(own_key, extent, shards, smallest, high):
    def one(position, shards_of):
        steps = jax.random.uniform(jax.random.fold_in(jax.random.fold_in(own_key, 6), position), (shards_of,), jnp.float32, smallest / len(shards), high / len(shards))
        return jnp.repeat(jnp.exp(steps), extent[position] // shards_of).reshape((-1,) + (1,) * (len(extent) - position - 1))

    loudness = one(*shards[0])
    for cut in shards[1:]:
        loudness = loudness * one(*cut)
    return loudness


def bell_draw(rng, extent, scale, bound, cuts=(), held_as=jnp.bfloat16):
    drawn = scale * jax.random.normal(rng, extent, jnp.float32)
    if cuts:
        drawn = drawn * shard_levels(rng, extent, cuts, -0.22, 0.18)
    return jnp.clip(drawn, -bound, bound).astype(held_as)


def setup_inputs(seed: int = 0) -> dict:
    arg_keys = jax.random.split(jax.random.key(seed), 13)
    return {
        "populations": draw_populations(jax.random.fold_in(arg_keys[12], 71), 0),
        "le_offset": jax.random.randint(arg_keys[1], (1,), 0, NX).astype(jnp.int32),
        "sphere_velocity": bell_draw(arg_keys[2], (3, N_FLOW, N_GRAD, SPH_DEV), 0.1, 0.4, ((1, 16), (2, 16)), jnp.float32),
        "link_cell": draw_link_cell(jax.random.fold_in(arg_keys[12], 71), 0),
        "link_dir": draw_link_dir(jax.random.fold_in(arg_keys[12], 71), 0),
        "link_sphere": plant(jax.random.randint(arg_keys[5], (N_FLOW, N_GRAD, LINKS_DEV), 0, 9 * SPH_DEV), jax.random.fold_in(arg_keys[5], 1), 0, (9 * SPH_DEV) - 1).astype(jnp.int32),
        "link_count": draw_link_count(jax.random.fold_in(arg_keys[12], 71), 0),
        "pair_first": plant(jax.random.randint(arg_keys[7], (N_FLOW, N_GRAD, PAIRS_DEV), 0, SPH_DEV), jax.random.fold_in(arg_keys[7], 1), 0, SPH_DEV - 1).astype(jnp.int32),
        "pair_second": plant(jax.random.randint(arg_keys[8], (N_FLOW, N_GRAD, PAIRS_DEV), 0, 9 * SPH_DEV), jax.random.fold_in(arg_keys[8], 1), 0, (9 * SPH_DEV) - 1).astype(jnp.int32),
        "pair_count": draw_pair_count(jax.random.fold_in(arg_keys[12], 71), 0),
        "pair_gap": jnp.clip(0.02 + 0.98 * jax.random.uniform(arg_keys[10], (N_FLOW, N_GRAD, PAIRS_DEV), jnp.float32) ** shard_levels(arg_keys[10], (N_FLOW, N_GRAD, PAIRS_DEV), ((0, 16), (1, 16)), -0.2, 0.2), 0.02, 1.0),
        "pair_normal": draw_pair_normal(jax.random.fold_in(arg_keys[12], 71), 0),
    }


VELOCITIES = [(0, 0, 0), (1, 0, 0), (-1, 0, 0), (0, 1, 0), (0, -1, 0), (0, 0, 1), (0, 0, -1), (1, 1, 0), (-1, -1, 0), (1, -1, 0), (-1, 1, 0), (1, 0, 1), (-1, 0, -1), (1, 0, -1), (-1, 0, 1), (0, 1, 1), (0, -1, -1), (0, 1, -1), (0, -1, 1)]
WEIGHTS = [1.0 / 3.0] + [1.0 / 18.0] * 6 + [1.0 / 36.0] * 12
RELAX_TIME = 0.8
SHEAR_SPEED = 0.1
LUB_COEF = 0.5
GAP_FLOOR = 0.1
GAP_CUTOFF = 1.0
INV_MASS = 1.0 / 523.6


def collide(populations):
    density = jnp.sum(populations, axis=0)
    speeds = []
    for axis_id in range(3):
        running = None
        for direction, vector in enumerate(VELOCITIES):
            if vector[axis_id] != 0:
                addend = vector[axis_id] * populations[direction]
                running = addend if running is None else running + addend
        speeds.append(running / density)
    speed_sq = speeds[0] * speeds[0] + speeds[1] * speeds[1] + speeds[2] * speeds[2]
    relaxed = []
    for direction, vector in enumerate(VELOCITIES):
        c_dot = None
        for axis_id in range(3):
            if vector[axis_id] != 0:
                addend = vector[axis_id] * speeds[axis_id]
                c_dot = addend if c_dot is None else c_dot + addend
        if c_dot is None:
            equil = WEIGHTS[direction] * density * (1.0 - 1.5 * speed_sq)
        else:
            equil = WEIGHTS[direction] * density * (1.0 + 3.0 * c_dot + 4.5 * c_dot * c_dot - 1.5 * speed_sq)
        current = populations[direction]
        relaxed.append(current - (current - equil) / RELAX_TIME)
    return relaxed, density


def tile_links(relaxed, density, propagated, near_speed, link_cell, link_dir, link_sphere, link_count, pair_first, pair_second, pair_count, pair_gap, pair_normal):
    n_cells = relaxed.shape[1]
    slot_count = near_speed.shape[1] // 9
    onehot = (link_dir[None, :] == lax.iota(jnp.int32, 19)[:, None]).astype(relaxed.dtype)
    lookup = jnp.asarray([[vector[k] for vector in VELOCITIES] for k in range(3)] + [WEIGHTS], relaxed.dtype)
    picked = jnp.dot(lookup, onehot, precision=lax.Precision.HIGHEST)
    leaving = jnp.sum(onehot * relaxed[:, link_cell], axis=0)
    wall_speed = near_speed[:, link_sphere]
    c_dot_u = jnp.sum(picked[:3] * wall_speed, axis=0)
    bounced = leaving - 6.0 * picked[3] * density[link_cell] * c_dot_u
    is_live = lax.iota(jnp.int32, link_dir.shape[0]) < link_count
    opposite = jnp.where(link_dir % 2 == 1, link_dir + 1, link_dir - 1)
    target = jnp.where(is_live, opposite * n_cells + link_cell, 19 * n_cells)
    updated = propagated.reshape(-1).at[target].set(bounced, mode="drop").reshape(19, n_cells)
    link_force = picked[:3] * (leaving + bounced) * is_live.astype(relaxed.dtype)
    pair_live = (lax.iota(jnp.int32, pair_first.shape[0]) < pair_count).astype(relaxed.dtype)
    first_ref = pair_first + 4 * slot_count
    first_speed = near_speed[:, first_ref]
    second_speed = near_speed[:, pair_second]
    normal_rate = jnp.sum((first_speed - second_speed) * pair_normal, axis=0)
    resist = LUB_COEF * (1.0 / jnp.maximum(pair_gap, GAP_FLOOR) - 1.0 / GAP_CUTOFF)
    lubrication = -resist * normal_rate * pair_normal * pair_live
    sphere_refs = jnp.concatenate([link_sphere, first_ref, pair_second])
    values = jnp.concatenate([link_force, lubrication, -lubrication], axis=1)
    partial_value = jax.ops.segment_sum(values.T, sphere_refs, num_segments=9 * slot_count).T
    return updated, partial_value


def reference(populations, le_offset, sphere_velocity, link_cell, link_dir, link_sphere, link_count, pair_first, pair_second, pair_count, pair_gap, pair_normal):
    relaxed, density = collide(populations)
    offset_cells = le_offset[0]
    moved = []
    for direction, vector in enumerate(VELOCITIES):
        layer = relaxed[direction]
        boost = 6.0 * WEIGHTS[direction] * vector[0] * SHEAR_SPEED
        below = jnp.roll(layer[:, NY - 1, :], -offset_cells, axis=0) - boost
        above = jnp.roll(layer[:, 0, :], offset_cells, axis=0) + boost
        padded = jnp.concatenate([below[:, None, :], layer, above[:, None, :]], axis=1)
        rows_kept = padded[:, 1 - vector[1]:1 - vector[1] + NY, :]
        moved.append(jnp.roll(rows_kept, (vector[0], vector[2]), axis=(0, 2)))
    tiles = N_FLOW * N_GRAD
    cells_tile = CX * CY * NZ

    def to_tiles(field, count):
        return field.reshape(count, N_FLOW, CX, N_GRAD, CY, NZ).transpose(1, 3, 0, 2, 4, 5).reshape(tiles, count, cells_tile)

    relaxed_tiles = to_tiles(jnp.stack(relaxed), 19)
    moved_tiles = to_tiles(jnp.stack(moved), 19)
    density_tiles = to_tiles(density[None], 1)[:, 0]
    rolled = []
    for code in range(9):
        rolled.append(jnp.roll(sphere_velocity, (1 - code // 3, 1 - code % 3), axis=(1, 2)))
    near_speed = jnp.stack(rolled).transpose(2, 3, 1, 0, 4).reshape(tiles, 3, 9 * SPH_DEV)
    inputs = (relaxed_tiles, density_tiles, moved_tiles, near_speed,
              link_cell.reshape(tiles, LINKS_DEV), link_dir.reshape(tiles, LINKS_DEV),
              link_sphere.reshape(tiles, LINKS_DEV), link_count.reshape(tiles),
              pair_first.reshape(tiles, PAIRS_DEV), pair_second.reshape(tiles, PAIRS_DEV),
              pair_count.reshape(tiles), pair_gap.reshape(tiles, PAIRS_DEV),
              pair_normal.transpose(1, 2, 0, 3).reshape(tiles, 3, PAIRS_DEV))
    updated, partials = lax.map(lambda pieces: tile_links(*pieces), inputs)
    populations_next = updated.reshape(N_FLOW, N_GRAD, 19, CX, CY, NZ).transpose(2, 0, 3, 1, 4, 5).reshape(19, NX, NY, NZ)
    partials = partials.reshape(N_FLOW, N_GRAD, 3, 9, SPH_DEV)
    accumulated = None
    for code in range(9):
        addend = jnp.roll(partials[:, :, :, code], (code // 3 - 1, code % 3 - 1), axis=(0, 1))
        accumulated = addend if accumulated is None else accumulated + addend
    sphere_force = accumulated.transpose(2, 0, 1, 3)
    velocity_next = sphere_velocity + INV_MASS * sphere_force
    return populations_next, sphere_force, velocity_next
```

```python
import functools

import jax
import jax.numpy as jnp
from jax import lax
from jax.experimental import pallas as pl
from jax.experimental.pallas import tpu as pltpu
from jax.sharding import PartitionSpec as P

MESH = pl.DeviceIdType.MESH
VELOCITIES = [
    (0, 0, 0),
    (1, 0, 0),
    (-1, 0, 0),
    (0, 1, 0),
    (0, -1, 0),
    (0, 0, 1),
    (0, 0, -1),
    (1, 1, 0),
    (-1, -1, 0),
    (1, -1, 0),
    (-1, 1, 0),
    (1, 0, 1),
    (-1, 0, -1),
    (1, 0, -1),
    (-1, 0, 1),
    (0, 1, 1),
    (0, -1, -1),
    (0, 1, -1),
    (0, -1, 1),
]
WEIGHTS = [1.0 / 3.0] + [1.0 / 18.0] * 6 + [1.0 / 36.0] * 12
UPWARD = [3, 7, 10, 15, 17]
DOWNWARD = [4, 8, 9, 16, 18]
RIGHTWARD = [1, 7, 9, 11, 13]
LEFTWARD = [2, 8, 10, 12, 14]
RELAX_TIME = 0.8
SHEAR_SPEED = 0.1
LUB_COEF = 0.5
GAP_FLOOR = 0.1
GAP_CUTOFF = 1.0
INV_MASS = 1.0 / 523.6

LANES = 128
ROWS = 18 * 64
PAD = 64
REF_BITS = 10
DEAD = 1 << 30
LINK_ROWS = 128
SUM_ROWS = LINK_ROWS + 8


def iota(shape, dim):
    return lax.broadcasted_iota(jnp.int32, shape, dim)


def take(table, lanes):
    return jnp.take_along_axis(table, lanes, axis=1, mode="promise_in_bounds")


def collide(current):
    density = current[0]
    for direction in range(1, 19):
        density = density + current[direction]
    inverse = 1.0 / density
    speeds = []
    for axis_id in range(3):
        running = None
        for direction, vector in enumerate(VELOCITIES):
            if vector[axis_id] == 0:
                continue
            value = current[direction]
            if running is None:
                running = value
            elif vector[axis_id] > 0:
                running = running + value
            else:
                running = running - value
        speeds.append(running * inverse)
    speed_sq = speeds[0] * speeds[0] + speeds[1] * speeds[1] + speeds[2] * speeds[2]
    common = 1.0 - 1.5 * speed_sq
    kept = 1.0 - 1.0 / RELAX_TIME
    relaxed = [kept * current[0] + (WEIGHTS[0] / RELAX_TIME) * density * common]
    scaled = {}
    for direction in range(1, 19, 2):
        vector = VELOCITIES[direction]
        weight = WEIGHTS[direction]
        if weight not in scaled:
            scaled[weight] = (weight / RELAX_TIME) * density
        c_dot = None
        for axis_id in range(3):
            if vector[axis_id] != 0:
                term = speeds[axis_id]
                if c_dot is None:
                    c_dot = term
                elif vector[axis_id] > 0:
                    c_dot = c_dot + term
                else:
                    c_dot = c_dot - term
        even = scaled[weight] * (common + 4.5 * c_dot * c_dot)
        odd = scaled[weight] * (3.0 * c_dot)
        relaxed.append(kept * current[direction] + (even + odd))
        relaxed.append(kept * current[direction + 1] + (even - odd))
    return relaxed, density


def bitonic_sort(keys):
    place = iota((16, 8, 128), 0) + 16 * iota((16, 8, 128), 1) + 128 * iota((16, 8, 128), 2)
    sublane = iota((16, 8, 128), 1)
    lane = iota((128, 128), 1)
    for phase in range(1, 15):
        flips = place >> (phase - 1)
        if phase == 1:
            flips = place >> 1
        elif phase < 14:
            flips = flips ^ (place >> phase)
        keys = keys ^ (-(flips & 1))
        for bit in range(phase - 1, -1, -1):
            if bit < 4:
                step = 1 << bit
                pairs = keys.reshape(8 >> bit, 2, step, 8, 128)
                first, second = pairs[:, 0], pairs[:, 1]
                low, high = jnp.minimum(first, second), jnp.maximum(first, second)
                keys = jnp.stack([low, high], axis=1).reshape(16, 8, 128)
            elif bit < 7:
                step = 1 << (bit - 4)
                upper = (sublane & step) != 0
                partner = pltpu.roll(keys, step, 1)
                if step != 4:
                    partner = jnp.where(upper, partner, pltpu.roll(keys, 8 - step, 1))
                keys = jnp.where(upper, jnp.maximum(keys, partner), jnp.minimum(keys, partner))
            else:
                step = 1 << (bit - 7)
                flat = keys.reshape(128, 128)
                partner = take(flat, lane ^ step)
                upper = (lane & step) != 0
                flat = jnp.where(upper, jnp.maximum(flat, partner), jnp.minimum(flat, partner))
                keys = flat.reshape(16, 8, 128)
    return keys


def step_kernel(
    n_flow,
    n_grad,
    offset_ref,
    link_count_ref,
    pair_count_ref,
    pop_ref,
    velocity_ref,
    cell_ref,
    dir_ref,
    sphere_ref,
    first_ref,
    second_ref,
    gap_ref,
    normal_ref,
    next_ref,
    force_ref,
    moved_ref,
    relaxed,
    density,
    face_right,
    face_left,
    face_up,
    face_down,
    from_left,
    from_right,
    from_below,
    from_above,
    own_speed,
    near,
    speed_rows,
    sorted_keys,
    spread,
    strength,
    pair_ints,
    pair_floats,
    sum_code,
    sum_slot,
    sum_piece,
    part_out,
    part_in,
    face_send,
    face_recv,
    up_send,
    up_recv,
    down_send,
    down_recv,
    speed_send,
    speed_recv,
    part_send,
    part_recv,
):
    flow, grad = lax.axis_index("flow"), lax.axis_index("grad")
    right, left = lax.rem(flow + 1, n_flow), lax.rem(flow + n_flow - 1, n_flow)
    above, below = lax.rem(grad + 1, n_grad), lax.rem(grad + n_grad - 1, n_grad)
    up_targets = jnp.where(grad == n_grad - 1, n_flow, 3)
    down_targets = jnp.where(grad == 0, n_flow, 3)

    def column(step):
        return lax.rem(flow + n_flow - 1 + step, n_flow)

    barrier = pltpu.get_barrier_semaphore()
    for target in (left, right):
        pl.semaphore_signal(barrier, inc=1, device_id=(target, grad), device_id_type=MESH)

    def greet_up(step, carry):
        pl.semaphore_signal(barrier, inc=1, device_id=(column(step), above), device_id_type=MESH)
        return carry

    def greet_down(step, carry):
        pl.semaphore_signal(barrier, inc=1, device_id=(column(step), below), device_id_type=MESH)
        return carry

    lax.fori_loop(0, up_targets, greet_up, 0)
    lax.fori_loop(0, down_targets, greet_down, 0)

    for axis_id in range(3):
        own_speed[axis_id : axis_id + 1, 0:64] = velocity_ref[axis_id, 0]

    def collide_slab(x, carry):
        rows = pl.ds(pl.multiple_of(x * 8, 8), 8)
        values, total = collide([pop_ref[direction, x] for direction in range(19)])
        for direction in range(19):
            relaxed[direction, rows, :] = values[direction]
        density[rows, :] = total
        return carry

    lax.fori_loop(0, 8, collide_slab, 0)
    for slot in range(5):
        face_right[slot] = relaxed[RIGHTWARD[slot], 56:64, :]
        face_left[slot] = relaxed[LEFTWARD[slot], 0:8, :]
        face_up[slot] = relaxed[UPWARD[slot], pl.ds(7, 8, stride=8), :]
        face_down[slot] = relaxed[DOWNWARD[slot], pl.ds(0, 8, stride=8), :]

    pl.semaphore_wait(barrier, 2 + up_targets + down_targets)

    def speed_copy(code):
        target = (
            lax.rem(flow + n_flow - (code // 3 - 1), n_flow),
            lax.rem(grad + n_grad - (code % 3 - 1), n_grad),
        )
        return pltpu.make_async_remote_copy(
            src_ref=own_speed,
            dst_ref=near.at[code],
            send_sem=speed_send.at[code],
            recv_sem=speed_recv.at[code],
            device_id=target,
            device_id_type=MESH,
        )

    def part_copy(code):
        target = (
            lax.rem(flow + n_flow + (code // 3 - 1), n_flow),
            lax.rem(grad + n_grad + (code % 3 - 1), n_grad),
        )
        return pltpu.make_async_remote_copy(
            src_ref=part_out.at[code],
            dst_ref=part_in.at[code],
            send_sem=part_send.at[code],
            recv_sem=part_recv.at[code],
            device_id=target,
            device_id_type=MESH,
        )

    neighbours = [code for code in range(9) if code != 4]

    def face_copies():
        return (
            pltpu.make_async_remote_copy(
                src_ref=face_right,
                dst_ref=from_left,
                send_sem=face_send.at[0],
                recv_sem=face_recv.at[0],
                device_id=(right, grad),
                device_id_type=MESH,
            ),
            pltpu.make_async_remote_copy(
                src_ref=face_left,
                dst_ref=from_right,
                send_sem=face_send.at[1],
                recv_sem=face_recv.at[1],
                device_id=(left, grad),
                device_id_type=MESH,
            ),
        )

    def up_copy(target, source):
        return pltpu.make_async_remote_copy(
            src_ref=face_up,
            dst_ref=from_below.at[:, pl.ds(pl.multiple_of(source * 8, 8), 8), :],
            send_sem=up_send.at[target],
            recv_sem=up_recv.at[source],
            device_id=(target, above),
            device_id_type=MESH,
        )

    def down_copy(target, source):
        return pltpu.make_async_remote_copy(
            src_ref=face_down,
            dst_ref=from_above.at[:, pl.ds(pl.multiple_of(source * 8, 8), 8), :],
            send_sem=down_send.at[target],
            recv_sem=down_recv.at[source],
            device_id=(target, below),
            device_id_type=MESH,
        )

    def send_up(step, carry):
        up_copy(column(step), flow).start()
        return carry

    def send_down(step, carry):
        down_copy(column(step), flow).start()
        return carry

    lax.fori_loop(0, up_targets, send_up, 0)
    lax.fori_loop(0, down_targets, send_down, 0)
    for copy in face_copies():
        copy.start()
    for code in neighbours:
        speed_copy(code).start()

    number = iota((128, 128), 0) * 128 + iota((128, 128), 1)
    packed = (((dir_ref[...] - 1) * 8192 + cell_ref[...]) << REF_BITS) + sphere_ref[...]
    packed = jnp.where(number < link_count_ref[0, 0], packed, DEAD)
    ordered = bitonic_sort(packed.reshape(16, 8, 128))
    sorted_keys[...] = ordered.reshape(128, 128)
    picked = [sorted_keys[pl.ds(sublane, 16, stride=8), :] for sublane in range(8)]
    natural = jnp.transpose(jnp.concatenate(picked, axis=0))
    sorted_keys[...] = natural
    lag = natural - (number << REF_BITS)
    rest = lag & ((1 << 24) - 1)
    home = lag >> 24
    nothing = jnp.full((PAD, 128), -1, jnp.int32)
    for level in range(15):
        spread[level, 0:PAD, :] = nothing
    for block in range(9):
        spread[14, PAD + block * 128 : PAD + block * 128 + 128, :] = jnp.where(home == block, rest, -1)
    lane = iota((128, 128), 1)

    def spread_level(bit):
        unit = 1 << (bit + REF_BITS)

        def block_of(block, carry):
            base = pl.multiple_of(block * 128, 128)
            here = spread[bit + 1, pl.ds(base + PAD, 128), :]
            if bit >= 7:
                coming = spread[bit + 1, pl.ds(base + (PAD - (1 << (bit - 7))), 128), :]
            else:
                before = spread[bit + 1, pl.ds(base + (PAD - 1), 128), :]
                coming = pltpu.roll(jnp.where(lane >= 128 - (1 << bit), before, here), 1 << bit, 1)
            stays = jnp.where(here < unit, here, -1)
            spread[bit, pl.ds(base + PAD, 128), :] = jnp.where(coming >= unit, coming - unit, stays)
            return carry

        lax.fori_loop(0, 9, block_of, 0)

    for bit in range(13, -1, -1):
        spread_level(bit)

    for code in neighbours:
        speed_copy(code).wait_recv()
    near[4] = own_speed[...]
    half = iota((8, 128), 1) < 64
    for pair in range(5):
        row = near[2 * pair]
        if pair < 4:
            row = jnp.where(half, row, pltpu.roll(near[2 * pair + 1], 64, 1))
        for axis_id in range(3):
            speed_rows[45 + 5 * axis_id + pair : 46 + 5 * axis_id + pair, :] = row[axis_id : axis_id + 1]
        for line in range(9):
            vector = VELOCITIES[2 * line + 1]
            total = None
            for axis_id in range(3):
                if vector[axis_id] != 0:
                    term = row[axis_id : axis_id + 1]
                    if total is None:
                        total = term
                    elif vector[axis_id] > 0:
                        total = total + term
                    else:
                        total = total - term
            speed_rows[5 * line + pair : 5 * line + pair + 1, :] = total

    def speed_of(line, refs):
        lanes = refs & 127
        group = refs >> 7
        found = take(jnp.broadcast_to(speed_rows[5 * line : 5 * line + 1, :], refs.shape), lanes)
        for pair in range(1, 5):
            row = jnp.broadcast_to(speed_rows[5 * line + pair : 5 * line + pair + 1, :], refs.shape)
            found = jnp.where(group == pair, take(row, lanes), found)
        return found

    def came_up(step, carry):
        up_copy(column(step), column(step)).wait_recv()
        return carry

    def came_down(step, carry):
        down_copy(column(step), column(step)).wait_recv()
        return carry

    lax.fori_loop(0, down_targets, came_up, 0)
    lax.fori_loop(0, up_targets, came_down, 0)
    for copy in face_copies():
        copy.wait_recv()

    span = 8 * n_flow
    offset = offset_ref[0]
    at_bottom, at_top = grad == 0, grad == n_grad - 1
    shift_below = jnp.where(at_bottom, offset, 0)
    shift_above = jnp.where(at_top, span - offset, 0)
    boost_below = jnp.where(at_bottom, -6.0 * SHEAR_SPEED, 0.0)
    boost_above = jnp.where(at_top, 6.0 * SHEAR_SPEED, 0.0)
    tall = iota((8, 128), 0)

    def propagated(direction):
        c_x, c_y, c_z = VELOCITIES[direction]
        slabs = []
        for x in range(8):
            source = x - c_x
            if c_x == 0 or 0 <= source < 8:
                slab = relaxed[direction, source * 8 : source * 8 + 8, :]
            elif c_x > 0:
                slab = from_left[RIGHTWARD.index(direction)]
            else:
                slab = from_right[LEFTWARD.index(direction)]
            if c_y != 0:
                rows_from, shift, boost = (from_below, shift_below, boost_below) if c_y > 0 else (from_above, shift_above, boost_above)
                slot = (UPWARD if c_y > 0 else DOWNWARD).index(direction)
                place = lax.rem(flow * 8 + (source + span) + shift, span)
                ghost = rows_from[slot, pl.ds(place, 1), :]
                if c_x != 0:
                    ghost = ghost + boost * (WEIGHTS[direction] * c_x)
                slab = pltpu.roll(slab, 1 if c_y > 0 else 7, 0)
                slab = jnp.where(tall == (0 if c_y > 0 else 7), jnp.broadcast_to(ghost, (8, 128)), slab)
            if c_z != 0:
                slab = pltpu.roll(slab, 1 if c_z > 0 else 127, 1)
            slabs.append(slab)
        return jnp.concatenate(slabs, axis=0)

    next_ref[0] = relaxed[0].reshape(8, 8, 128)
    for direction in range(1, 19):
        opposite = direction + 1 if direction % 2 == 1 else direction - 1
        sign = 1.0 if direction % 2 == 1 else -1.0
        refs = spread[0, PAD + 64 * (direction - 1) : PAD + 64 * direction, :]
        leaving = relaxed[direction]
        wall = speed_of((direction - 1) // 2, refs)
        bounced = leaving - (6.0 * WEIGHTS[direction] * sign) * density[...] * wall
        strength[0, 64 * (direction - 1) : 64 * direction, :] = leaving + bounced
        updated = jnp.where(refs >= 0, bounced, propagated(opposite))
        next_ref[opposite] = updated.reshape(8, 8, 128)

    def gather_level(bit):
        unit = 1 << (bit + REF_BITS)
        now, later = bit % 2, (bit + 1) % 2

        def block_of(block, carry):
            base = pl.multiple_of(block * 128, 128)
            moves = spread[bit + 1, pl.ds(base + PAD, 128), :] >= unit
            here = strength[now, pl.ds(base, 128), :]
            if bit >= 7:
                ahead = strength[now, pl.ds(base + (1 << (bit - 7)), 128), :]
            else:
                after = strength[now, pl.ds(base + 1, 128), :]
                ahead = pltpu.roll(jnp.where(lane < (1 << bit), after, here), 128 - (1 << bit), 1)
            strength[later, pl.ds(base, 128), :] = jnp.where(moves, ahead, here)
            return carry

        lax.fori_loop(0, 9, block_of, 0)

    for bit in range(14):
        gather_level(bit)
    keys = sorted_keys[...]
    lag = keys - (number << REF_BITS)
    home = lag >> 24
    push = jnp.zeros((128, 128), jnp.float32)
    for block in range(9):
        push = jnp.where(home == block, strength[0, block * 128 : block * 128 + 128, :], push)

    def put_terms(rows, refs, terms):
        sum_code[rows, :] = refs >> 6
        sum_slot[rows, :] = refs & 63
        for axis_id in range(3):
            coarse = terms[axis_id].astype(jnp.bfloat16).astype(jnp.float32)
            sum_piece[axis_id, rows, :] = coarse
            sum_piece[3 + axis_id, rows, :] = terms[axis_id] - coarse

    kind = (keys >> 23) & 127
    small_lane = iota((8, 128), 1)
    terms = []
    for axis_id in range(3):
        table = jnp.zeros((8, 128), jnp.float32)
        for direction in range(1, 19):
            part = VELOCITIES[direction][axis_id]
            if part != 0:
                table = jnp.where(small_lane == direction - 1, float(part), table)
        tall_table = jnp.concatenate([table] * 16, axis=0)
        terms.append(take(tall_table, kind) * push)
    put_terms(pl.ds(0, 128), keys & 1023, terms)

    pair_ints[...] = jnp.zeros((2, 8, 128), jnp.int32)
    pair_floats[...] = jnp.ones((4, 8, 128), jnp.float32)
    for row in range(2):
        lanes = slice(row * 128, row * 128 + 128)
        pair_ints[0, row : row + 1, :] = first_ref[0, :, lanes] + 256
        pair_ints[1, row : row + 1, :] = second_ref[0, :, lanes]
        pair_floats[3, row : row + 1, :] = gap_ref[0, :, lanes]
        for axis_id in range(3):
            pair_floats[axis_id, row : row + 1, :] = normal_ref[axis_id, 0, :, lanes]
    heads, tails = pair_ints[0], pair_ints[1]
    normals = [pair_floats[axis_id] for axis_id in range(3)]
    rate = None
    for axis_id in range(3):
        gap_speed = (speed_of(9 + axis_id, heads) - speed_of(9 + axis_id, tails)) * normals[axis_id]
        rate = gap_speed if rate is None else rate + gap_speed
    resist = LUB_COEF * (1.0 / jnp.maximum(pair_floats[3], GAP_FLOOR) - 1.0 / GAP_CUTOFF)
    alive = iota((8, 128), 0) * 128 + small_lane < jnp.minimum(pair_count_ref[0, 0], 256)
    scale = jnp.where(alive, -resist * rate, 0.0)
    lift = [scale * normals[axis_id] for axis_id in range(3)]
    lower = iota((8, 128), 0) < 2
    both = jnp.where(lower, heads, pltpu.roll(tails, 2, 0))
    lift = [jnp.where(lower, term, -pltpu.roll(term, 2, 0)) for term in lift]
    put_terms(pl.ds(128, 8), both, lift)

    code_rows = iota((16, 128), 0)
    slot_rows = iota((64, 128), 0)

    def add_rows(group, total):
        base = group * 8
        pieces, slots = [], []
        for row in range(8):
            at = pl.ds(base + row, 1)
            chosen = code_rows == jnp.broadcast_to(sum_code[at, :], (16, 128))
            parts = [
                jnp.where(chosen, jnp.broadcast_to(sum_piece[piece, at, :], (16, 128)), 0.0).astype(jnp.bfloat16)
                for piece in range(6)
            ]
            pieces.append(jnp.concatenate(parts, axis=0))
            slot = slot_rows == jnp.broadcast_to(sum_slot[at, :], (64, 128))
            slots.append(jnp.where(slot, 1.0, 0.0).astype(jnp.bfloat16))
        return total + lax.dot_general(
            jnp.concatenate(pieces, axis=1),
            jnp.concatenate(slots, axis=1),
            (((1,), (1,)), ((), ())),
            preferred_element_type=jnp.float32,
        )

    total = lax.fori_loop(0, SUM_ROWS // 8, add_rows, jnp.zeros((96, 64), jnp.float32))
    for axis_id in range(3):
        summed = total[16 * axis_id : 16 * axis_id + 16] + total[48 + 16 * axis_id : 64 + 16 * axis_id]
        for code in range(9):
            part_out[code, axis_id : axis_id + 1, 0:64] = summed[code : code + 1]

    for code in neighbours:
        part_copy(code).start()
    forces = part_out[4]
    for code in neighbours:
        part_copy(code).wait_recv()
        forces = forces + part_in[code]
    for axis_id in range(3):
        force = forces[axis_id : axis_id + 1, 0:64]
        force_ref[axis_id, 0] = force
        moved_ref[axis_id, 0] = velocity_ref[axis_id, 0] + INV_MASS * force

    for code in neighbours:
        part_copy(code).wait_send()
        speed_copy(code).wait_send()
    for copy in face_copies():
        copy.wait_send()

    def sent_up(step, carry):
        up_copy(column(step), flow).wait_send()
        return carry

    def sent_down(step, carry):
        down_copy(column(step), flow).wait_send()
        return carry

    lax.fori_loop(0, up_targets, sent_up, 0)
    lax.fori_loop(0, down_targets, sent_down, 0)


def per_device(
    n_flow,
    n_grad,
    populations,
    le_offset,
    sphere_velocity,
    link_cell,
    link_dir,
    link_sphere,
    link_count,
    pair_first,
    pair_second,
    pair_count,
    pair_gap,
    pair_normal,
):
    vmem = pl.BlockSpec(memory_space=pltpu.VMEM)
    smem = pl.BlockSpec(memory_space=pltpu.SMEM)
    span = 8 * n_flow
    f32, i32 = jnp.float32, jnp.int32
    dma = pltpu.SemaphoreType.DMA
    return pl.pallas_call(
        functools.partial(step_kernel, n_flow, n_grad),
        out_shape=(
            jax.ShapeDtypeStruct(populations.shape, f32),
            jax.ShapeDtypeStruct(sphere_velocity.shape, f32),
            jax.ShapeDtypeStruct(sphere_velocity.shape, f32),
        ),
        in_specs=[smem] * 3 + [vmem] * 9,
        out_specs=(vmem, vmem, vmem),
        scratch_shapes=[
            pltpu.VMEM((19, 64, 128), f32),
            pltpu.VMEM((64, 128), f32),
            pltpu.VMEM((5, 8, 128), f32),
            pltpu.VMEM((5, 8, 128), f32),
            pltpu.VMEM((5, 8, 128), f32),
            pltpu.VMEM((5, 8, 128), f32),
            pltpu.VMEM((5, 8, 128), f32),
            pltpu.VMEM((5, 8, 128), f32),
            pltpu.VMEM((5, span, 128), f32),
            pltpu.VMEM((5, span, 128), f32),
            pltpu.VMEM((8, 128), f32),
            pltpu.VMEM((9, 8, 128), f32),
            pltpu.VMEM((64, 128), f32),
            pltpu.VMEM((128, 128), i32),
            pltpu.VMEM((15, PAD + ROWS, 128), i32),
            pltpu.VMEM((2, ROWS + PAD, 128), f32),
            pltpu.VMEM((2, 8, 128), i32),
            pltpu.VMEM((4, 8, 128), f32),
            pltpu.VMEM((SUM_ROWS, 128), i32),
            pltpu.VMEM((SUM_ROWS, 128), i32),
            pltpu.VMEM((6, SUM_ROWS, 128), f32),
            pltpu.VMEM((9, 8, 128), f32),
            pltpu.VMEM((9, 8, 128), f32),
            dma((2,)),
            dma((2,)),
            dma((n_flow,)),
            dma((n_flow,)),
            dma((n_flow,)),
            dma((n_flow,)),
            dma((9,)),
            dma((9,)),
            dma((9,)),
            dma((9,)),
        ],
        compiler_params=pltpu.CompilerParams(
            collective_id=0, has_side_effects=True, vmem_limit_bytes=40 * 1024 * 1024
        ),
        name="lattice_step",
    )(
        le_offset,
        link_count,
        pair_count,
        populations,
        sphere_velocity,
        link_cell.reshape(128, 128),
        link_dir.reshape(128, 128),
        link_sphere.reshape(128, 128),
        pair_first,
        pair_second,
        pair_gap,
        pair_normal,
    )


def solution(mesh):
    tiled = P(None, "flow", "grad", None)
    listed = P("flow", "grad", None)
    counted = P("flow", "grad")
    return jax.shard_map(
        functools.partial(per_device, mesh.shape["flow"], mesh.shape["grad"]),
        mesh=mesh,
        in_specs=(tiled, P(), tiled, listed, listed, listed, counted, listed, listed, counted, listed, tiled),
        out_specs=(tiled, tiled, tiled),
        check_vma=False,
    )
```

```python
import functools

import jax
import jax.numpy as jnp
from jax import lax
from jax.experimental import pallas as pl
from jax.experimental.pallas import tpu as pltpu
from jax.sharding import PartitionSpec as P

MESH = pl.DeviceIdType.MESH
VELOCITIES = [
    (0, 0, 0),
    (1, 0, 0),
    (-1, 0, 0),
    (0, 1, 0),
    (0, -1, 0),
    (0, 0, 1),
    (0, 0, -1),
    (1, 1, 0),
    (-1, -1, 0),
    (1, -1, 0),
    (-1, 1, 0),
    (1, 0, 1),
    (-1, 0, -1),
    (1, 0, -1),
    (-1, 0, 1),
    (0, 1, 1),
    (0, -1, -1),
    (0, 1, -1),
    (0, -1, 1),
]
WEIGHTS = [1.0 / 3.0] + [1.0 / 18.0] * 6 + [1.0 / 36.0] * 12
UPWARD = [3, 7, 10, 15, 17]
DOWNWARD = [4, 8, 9, 16, 18]
RIGHTWARD = [1, 7, 9, 11, 13]
LEFTWARD = [2, 8, 10, 12, 14]
RELAX_TIME = 0.8
SHEAR_SPEED = 0.1
LUB_COEF = 0.5
GAP_FLOOR = 0.1
GAP_CUTOFF = 1.0
INV_MASS = 1.0 / 523.6

REF_BITS = 10
LANE_UNROLL = 16
ROW_UNROLL = 9
BACK_LANE_UNROLL = 8
BACK_ROW_UNROLL = 9
SUM_UNROLL = 17
DEAD = 1 << 30
LINK_ROWS = 128
SUM_ROWS = LINK_ROWS + 8


def iota(shape, dim):
    return lax.broadcasted_iota(jnp.int32, shape, dim)


def take(table, lanes):
    return jnp.take_along_axis(table, lanes, axis=1, mode="promise_in_bounds")


def collide(current):
    density = current[0]
    for direction in range(1, 19):
        density = density + current[direction]
    inverse = 1.0 / density
    speeds = []
    for axis_id in range(3):
        running = None
        for direction, vector in enumerate(VELOCITIES):
            if vector[axis_id] == 0:
                continue
            value = current[direction]
            if running is None:
                running = value
            elif vector[axis_id] > 0:
                running = running + value
            else:
                running = running - value
        speeds.append(running * inverse)
    speed_sq = speeds[0] * speeds[0] + speeds[1] * speeds[1] + speeds[2] * speeds[2]
    common = 1.0 - 1.5 * speed_sq
    kept = 1.0 - 1.0 / RELAX_TIME
    relaxed = [kept * current[0] + (WEIGHTS[0] / RELAX_TIME) * density * common]
    scaled = {}
    for direction in range(1, 19, 2):
        vector = VELOCITIES[direction]
        weight = WEIGHTS[direction]
        if weight not in scaled:
            scaled[weight] = (weight / RELAX_TIME) * density
        c_dot = None
        for axis_id in range(3):
            if vector[axis_id] != 0:
                term = speeds[axis_id]
                if c_dot is None:
                    c_dot = term
                elif vector[axis_id] > 0:
                    c_dot = c_dot + term
                else:
                    c_dot = c_dot - term
        even = scaled[weight] * (common + 4.5 * c_dot * c_dot)
        odd = scaled[weight] * (3.0 * c_dot)
        relaxed.append(kept * current[direction] + (even + odd))
        relaxed.append(kept * current[direction + 1] + (even - odd))
    return relaxed, density


def bitonic_sort(keys):
    place = iota((16, 8, 128), 0) + 16 * iota((16, 8, 128), 1) + 128 * iota((16, 8, 128), 2)
    sublane = iota((16, 8, 128), 1)
    lane = iota((128, 128), 1)
    for phase in range(1, 15):
        flips = place >> (phase - 1)
        if phase == 1:
            flips = place >> 1
        elif phase < 14:
            flips = flips ^ (place >> phase)
        keys = keys ^ (-(flips & 1))
        for bit in range(phase - 1, -1, -1):
            if bit < 4:
                step = 1 << bit
                pairs = keys.reshape(8 >> bit, 2, step, 8, 128)
                first, second = pairs[:, 0], pairs[:, 1]
                low, high = jnp.minimum(first, second), jnp.maximum(first, second)
                keys = jnp.stack([low, high], axis=1).reshape(16, 8, 128)
            elif bit < 7:
                step = 1 << (bit - 4)
                upper = (sublane & step) != 0
                partner = pltpu.roll(keys, step, 1)
                if step != 4:
                    partner = jnp.where(upper, partner, pltpu.roll(keys, 8 - step, 1))
                keys = jnp.where(upper, jnp.maximum(keys, partner), jnp.minimum(keys, partner))
            else:
                step = 1 << (bit - 7)
                flat = keys.reshape(128, 128)
                partner = take(flat, lane ^ step)
                upper = (lane & step) != 0
                flat = jnp.where(upper, jnp.maximum(flat, partner), jnp.minimum(flat, partner))
                keys = flat.reshape(16, 8, 128)
    return keys


def step_kernel(
    n_flow,
    n_grad,
    offset_ref,
    link_count_ref,
    pair_count_ref,
    pop_hbm,
    velocity_hbm,
    cell_hbm,
    dir_hbm,
    sphere_hbm,
    first_hbm,
    second_hbm,
    gap_hbm,
    normal_hbm,
    next_ref,
    force_ref,
    moved_ref,
    pop_ref,
    velocity_ref,
    cell_ref,
    dir_ref,
    sphere_ref,
    first_ref,
    second_ref,
    gap_ref,
    normal_ref,
    in_sem,
    relaxed,
    density,
    face_right,
    face_left,
    face_up,
    face_down,
    from_left,
    from_right,
    from_below,
    from_above,
    own_speed,
    near,
    speed_rows,
    sorted_keys,
    rests,
    homes,
    spread,
    bounced,
    strength,
    rim,
    pushes,
    pair_ints,
    pair_floats,
    sum_code,
    sum_slot,
    sum_piece,
    part_out,
    part_in,
    face_send,
    face_recv,
    up_send,
    up_recv,
    down_send,
    down_recv,
    speed_send,
    speed_recv,
    part_send,
    part_recv,
):
    flow, grad = lax.axis_index("flow"), lax.axis_index("grad")
    right, left = lax.rem(flow + 1, n_flow), lax.rem(flow + n_flow - 1, n_flow)
    above, below = lax.rem(grad + 1, n_grad), lax.rem(grad + n_grad - 1, n_grad)
    up_targets = jnp.where(grad == n_grad - 1, n_flow, 3)
    down_targets = jnp.where(grad == 0, n_flow, 3)

    def column(step):
        return lax.rem(flow + n_flow - 1 + step, n_flow)

    copies_in = {}

    def bring(name, source, target):
        copies_in[name] = pltpu.make_async_copy(source, target, in_sem.at[len(copies_in)])
        copies_in[name].start()

    bring("velocity", velocity_hbm, velocity_ref)
    for x in range(8):
        bring(x, pop_hbm.at[:, x], pop_ref.at[:, x])
    bring("dir", dir_hbm, dir_ref)
    bring("cell", cell_hbm, cell_ref)
    bring("sphere", sphere_hbm, sphere_ref)
    bring("first", first_hbm, first_ref)
    bring("second", second_hbm, second_ref)
    bring("gap", gap_hbm, gap_ref)
    bring("normal", normal_hbm, normal_ref)

    barrier = pltpu.get_barrier_semaphore()
    for target in (left, right):
        pl.semaphore_signal(barrier, inc=1, device_id=(target, grad), device_id_type=MESH)

    def greet_up(step, carry):
        pl.semaphore_signal(barrier, inc=1, device_id=(column(step), above), device_id_type=MESH)
        return carry

    def greet_down(step, carry):
        pl.semaphore_signal(barrier, inc=1, device_id=(column(step), below), device_id_type=MESH)
        return carry

    lax.fori_loop(0, up_targets, greet_up, 0)
    lax.fori_loop(0, down_targets, greet_down, 0)

    copies_in["velocity"].wait()
    for axis_id in range(3):
        own_speed[axis_id : axis_id + 1, 0:64] = velocity_ref[axis_id, 0]

    def collide_slab(x, carry):
        rows = pl.ds(pl.multiple_of(x * 8, 8), 8)
        values, total = collide([pop_ref[direction, x] for direction in range(19)])
        for direction in range(19):
            relaxed[direction, rows, :] = values[direction]
        density[rows, :] = total
        return carry

    for x in range(8):
        copies_in[x].wait()
    lax.fori_loop(0, 8, collide_slab, 0)
    for slot in range(5):
        face_right[slot] = relaxed[RIGHTWARD[slot], 56:64, :]
        face_left[slot] = relaxed[LEFTWARD[slot], 0:8, :]
        face_up[slot] = relaxed[UPWARD[slot], pl.ds(7, 8, stride=8), :]
        face_down[slot] = relaxed[DOWNWARD[slot], pl.ds(0, 8, stride=8), :]

    def speed_copy(code):
        target = (
            lax.rem(flow + n_flow - (code // 3 - 1), n_flow),
            lax.rem(grad + n_grad - (code % 3 - 1), n_grad),
        )
        return pltpu.make_async_remote_copy(
            src_ref=own_speed,
            dst_ref=near.at[code],
            send_sem=speed_send.at[code],
            recv_sem=speed_recv.at[code],
            device_id=target,
            device_id_type=MESH,
        )

    def part_copy(code):
        target = (
            lax.rem(flow + n_flow + (code // 3 - 1), n_flow),
            lax.rem(grad + n_grad + (code % 3 - 1), n_grad),
        )
        return pltpu.make_async_remote_copy(
            src_ref=part_out.at[code],
            dst_ref=part_in.at[code],
            send_sem=part_send.at[code],
            recv_sem=part_recv.at[code],
            device_id=target,
            device_id_type=MESH,
        )

    neighbours = [code for code in range(9) if code != 4]

    def face_copies():
        return (
            pltpu.make_async_remote_copy(
                src_ref=face_right,
                dst_ref=from_left,
                send_sem=face_send.at[0],
                recv_sem=face_recv.at[0],
                device_id=(right, grad),
                device_id_type=MESH,
            ),
            pltpu.make_async_remote_copy(
                src_ref=face_left,
                dst_ref=from_right,
                send_sem=face_send.at[1],
                recv_sem=face_recv.at[1],
                device_id=(left, grad),
                device_id_type=MESH,
            ),
        )

    def up_copy(target, source):
        return pltpu.make_async_remote_copy(
            src_ref=face_up,
            dst_ref=from_below.at[:, pl.ds(pl.multiple_of(source * 8, 8), 8), :],
            send_sem=up_send.at[target],
            recv_sem=up_recv.at[source],
            device_id=(target, above),
            device_id_type=MESH,
        )

    def down_copy(target, source):
        return pltpu.make_async_remote_copy(
            src_ref=face_down,
            dst_ref=from_above.at[:, pl.ds(pl.multiple_of(source * 8, 8), 8), :],
            send_sem=down_send.at[target],
            recv_sem=down_recv.at[source],
            device_id=(target, below),
            device_id_type=MESH,
        )

    def send_up(step, carry):
        up_copy(column(step), flow).start()
        return carry

    def send_down(step, carry):
        down_copy(column(step), flow).start()
        return carry

    def send_all():
        pl.semaphore_wait(barrier, 2 + up_targets + down_targets)
        for code in neighbours:
            speed_copy(code).start()
        for copy in face_copies():
            copy.start()
        lax.fori_loop(0, up_targets, send_up, 0)
        lax.fori_loop(0, down_targets, send_down, 0)

    sends_later = jnp.logical_and(jnp.logical_or(grad == 0, grad == n_grad - 1), flow < n_flow // 2)
    pl.when(jnp.logical_not(sends_later))(send_all)

    copies_in["dir"].wait()
    copies_in["cell"].wait()
    copies_in["sphere"].wait()
    kinds, cells = dir_ref[...] - 1, cell_ref[...]
    packed = ((kinds >> 1) << 24) | ((cells & 127) << 17) | ((kinds & 1) << 16) | ((cells >> 7) << REF_BITS) | sphere_ref[...]
    listed = iota((128, 128), 0) * 128 + iota((128, 128), 1)
    packed = jnp.where(listed < link_count_ref[0, 0], packed, DEAD)
    ordered = bitonic_sort(packed.reshape(16, 8, 128))
    sorted_keys[...] = ordered.reshape(128, 128)
    picked = [sorted_keys[pl.ds(sublane, 16, stride=8), :] for sublane in range(8)]
    natural = jnp.concatenate(picked, axis=0)
    sorted_keys[...] = natural
    number = iota((128, 128), 1) * 128 + iota((128, 128), 0)
    lag = natural - (number << REF_BITS)
    rests[...] = (lag & ((1 << 24) - 1)).reshape(16, 8, 128)
    homes[...] = (lag >> 24).reshape(16, 8, 128)
    for level in range(1, 8):
        spread[level, 0] = jnp.full((16, 8, 128), -1, jnp.int32)

    def advance(held, coming, unit):
        return jnp.where(coming >= unit, coming - unit, jnp.where(held < unit, held, -1))

    def spread_lanes(line, carry):
        rest, home = rests[line], homes[line]
        lane = iota((9, 8, 128), 2)
        edge = jnp.full((1, 8, 128), -1, jnp.int32)
        held = jnp.stack([jnp.where(home == block, rest, -1) for block in range(9)])
        for bit in range(13, 6, -1):
            spread[bit + 1, 1:10, line] = held
            step = 1 << (bit - 7)
            before = jnp.concatenate([edge, held[:8]], axis=0)
            coming = pltpu.roll(jnp.where(lane >= 128 - step, before, held), step, 2)
            held = advance(held, coming, 1 << (bit + REF_BITS))
        spread[7, 1:10, line] = held
        return carry

    lax.fori_loop(0, 16, spread_lanes, 0, unroll=LANE_UNROLL)

    def spread_rows(block, carry):
        sublane = iota((16, 8, 128), 1)
        held = spread[7, block + 1]
        for bit in range(6, -1, -1):
            if bit < 6:
                spread[bit + 1, block + 1] = held
            count = max(1 << bit, 8) // 8
            last = iota((count, 8, 128), 2) == 127
            around = jnp.where(last, spread[bit + 1, block, 16 - count : 16], held[16 - count :])
            before = jnp.concatenate([pltpu.roll(around, 1, 2), held[: 16 - count]], axis=0)
            if bit < 3:
                step = 1 << bit
                before = pltpu.roll(jnp.where(sublane >= 8 - step, before, held), step, 1)
            held = advance(held, before, 1 << (bit + REF_BITS))
        spread[0, block + 1] = held
        return carry

    lax.fori_loop(0, 9, spread_rows, 0, unroll=ROW_UNROLL)

    pl.when(sends_later)(send_all)

    for code in neighbours:
        speed_copy(code).wait_recv()
    near[4] = own_speed[...]
    half = iota((8, 128), 1) < 64
    for pair in range(5):
        row = near[2 * pair]
        if pair < 4:
            row = jnp.where(half, row, pltpu.roll(near[2 * pair + 1], 64, 1))
        for axis_id in range(3):
            speed_rows[45 + 5 * axis_id + pair : 46 + 5 * axis_id + pair, :] = row[axis_id : axis_id + 1]
        for line in range(9):
            vector = VELOCITIES[2 * line + 1]
            total = None
            for axis_id in range(3):
                if vector[axis_id] != 0:
                    term = row[axis_id : axis_id + 1]
                    if total is None:
                        total = term
                    elif vector[axis_id] > 0:
                        total = total + term
                    else:
                        total = total - term
            speed_rows[5 * line + pair : 5 * line + pair + 1, :] = total

    def speed_of(line, refs):
        lanes = refs & 127
        group = refs >> 7
        found = take(jnp.broadcast_to(speed_rows[5 * line : 5 * line + 1, :], refs.shape), lanes)
        for pair in range(1, 5):
            row = jnp.broadcast_to(speed_rows[5 * line + pair : 5 * line + pair + 1, :], refs.shape)
            found = jnp.where(group == pair, take(row, lanes), found)
        return found

    for direction in range(1, 19):
        sign = 1.0 if direction % 2 == 1 else -1.0
        pair, part = (direction - 1) // 2, (direction - 1) % 2
        refs = spread[0, 1 + pair, 8 * part : 8 * part + 8].reshape(64, 128)
        leaving = relaxed[direction]
        back = leaving - (6.0 * WEIGHTS[direction] * sign) * density[...] * speed_of(pair, refs)
        bounced[pair, 8 * part : 8 * part + 8] = back.reshape(8, 8, 128)
        strength[pair, 8 * part : 8 * part + 8] = (leaving + back).reshape(8, 8, 128)

    def gather_rows(turn, carry):
        block = 8 - turn
        sublane = iota((16, 8, 128), 1)
        held = strength[block]
        for bit in range(7):
            count = max(1 << bit, 8) // 8
            first = iota((count, 8, 128), 2) == 0
            around = jnp.where(first, rim[bit, 0:count], held[:count])
            rim[bit, 0:count] = held[:count]
            after = jnp.concatenate([held[count:], pltpu.roll(around, 127, 2)], axis=0)
            if bit < 3:
                step = 1 << bit
                after = pltpu.roll(jnp.where(sublane < step, after, held), 8 - step, 1)
            held = jnp.where(spread[bit + 1, block + 1] >= 1 << (bit + REF_BITS), after, held)
        strength[block] = held
        return carry

    lax.fori_loop(0, 9, gather_rows, 0, unroll=BACK_ROW_UNROLL)

    def gather_lanes(line, carry):
        lane = iota((9, 8, 128), 2)
        held = strength[:, line]
        for bit in range(7, 14):
            step = 1 << (bit - 7)
            after = jnp.concatenate([held[1:], held[8:]], axis=0)
            ahead = pltpu.roll(jnp.where(lane < step, after, held), 128 - step, 2)
            held = jnp.where(spread[bit + 1, 1:10, line] >= 1 << (bit + REF_BITS), ahead, held)
        home = homes[line]
        push = jnp.zeros((8, 128), jnp.float32)
        for block in range(9):
            push = jnp.where(home == block, held[block], push)
        pushes[line] = push
        return carry

    lax.fori_loop(0, 16, gather_lanes, 0, unroll=BACK_LANE_UNROLL)
    keys = sorted_keys[...]
    push = pushes[...].reshape(128, 128)

    def put_terms(rows, refs, terms):
        sum_code[rows, :] = refs >> 6
        sum_slot[rows, :] = refs & 63
        for axis_id in range(3):
            coarse = terms[axis_id].astype(jnp.bfloat16).astype(jnp.float32)
            sum_piece[axis_id, rows, :] = coarse
            sum_piece[3 + axis_id, rows, :] = terms[axis_id] - coarse

    kind = (((keys >> 24) << 1) | ((keys >> 16) & 1)) & 127
    small_lane = iota((8, 128), 1)
    terms = []
    for axis_id in range(3):
        table = jnp.zeros((8, 128), jnp.float32)
        for direction in range(1, 19):
            part = VELOCITIES[direction][axis_id]
            if part != 0:
                table = jnp.where(small_lane == direction - 1, float(part), table)
        tall_table = jnp.concatenate([table] * 16, axis=0)
        terms.append(take(tall_table, kind) * push)
    put_terms(pl.ds(0, 128), keys & 1023, terms)

    for name in ("first", "second", "gap", "normal"):
        copies_in[name].wait()
    pair_ints[...] = jnp.zeros((2, 8, 128), jnp.int32)
    pair_floats[...] = jnp.ones((4, 8, 128), jnp.float32)
    for row in range(2):
        lanes = slice(row * 128, row * 128 + 128)
        pair_ints[0, row : row + 1, :] = first_ref[0, :, lanes] + 256
        pair_ints[1, row : row + 1, :] = second_ref[0, :, lanes]
        pair_floats[3, row : row + 1, :] = gap_ref[0, :, lanes]
        for axis_id in range(3):
            pair_floats[axis_id, row : row + 1, :] = normal_ref[axis_id, 0, :, lanes]
    heads, tails = pair_ints[0], pair_ints[1]
    normals = [pair_floats[axis_id] for axis_id in range(3)]
    rate = None
    for axis_id in range(3):
        gap_speed = (speed_of(9 + axis_id, heads) - speed_of(9 + axis_id, tails)) * normals[axis_id]
        rate = gap_speed if rate is None else rate + gap_speed
    resist = LUB_COEF * (1.0 / jnp.maximum(pair_floats[3], GAP_FLOOR) - 1.0 / GAP_CUTOFF)
    alive = iota((8, 128), 0) * 128 + small_lane < jnp.minimum(pair_count_ref[0, 0], 256)
    scale = jnp.where(alive, -resist * rate, 0.0)
    lift = [scale * normals[axis_id] for axis_id in range(3)]
    lower = iota((8, 128), 0) < 2
    both = jnp.where(lower, heads, pltpu.roll(tails, 2, 0))
    lift = [jnp.where(lower, term, -pltpu.roll(term, 2, 0)) for term in lift]
    put_terms(pl.ds(128, 8), both, lift)

    code_rows = iota((16, 128), 0)
    slot_rows = iota((64, 128), 0)

    def add_rows(group, total):
        base = group * 8
        pieces, slots = [], []
        for row in range(8):
            at = pl.ds(base + row, 1)
            chosen = code_rows == jnp.broadcast_to(sum_code[at, :], (16, 128))
            parts = [
                jnp.where(chosen, jnp.broadcast_to(sum_piece[piece, at, :], (16, 128)), 0.0).astype(jnp.bfloat16)
                for piece in range(6)
            ]
            pieces.append(jnp.concatenate(parts, axis=0))
            slot = slot_rows == jnp.broadcast_to(sum_slot[at, :], (64, 128))
            slots.append(jnp.where(slot, 1.0, 0.0).astype(jnp.bfloat16))
        return total + lax.dot_general(
            jnp.concatenate(pieces, axis=1),
            jnp.concatenate(slots, axis=1),
            (((1,), (1,)), ((), ())),
            preferred_element_type=jnp.float32,
        )

    total = lax.fori_loop(0, SUM_ROWS // 8, add_rows, jnp.zeros((96, 64), jnp.float32), unroll=SUM_UNROLL)
    for axis_id in range(3):
        summed = total[16 * axis_id : 16 * axis_id + 16] + total[48 + 16 * axis_id : 64 + 16 * axis_id]
        for code in range(9):
            part_out[code, axis_id : axis_id + 1, 0:64] = summed[code : code + 1]

    for code in neighbours:
        part_copy(code).start()
    def came_up(step, carry):
        up_copy(column(step), column(step)).wait_recv()
        return carry

    def came_down(step, carry):
        down_copy(column(step), column(step)).wait_recv()
        return carry

    lax.fori_loop(0, down_targets, came_up, 0)
    lax.fori_loop(0, up_targets, came_down, 0)
    for copy in face_copies():
        copy.wait_recv()

    span = 8 * n_flow
    offset = offset_ref[0]
    at_bottom, at_top = grad == 0, grad == n_grad - 1
    shift_below = jnp.where(at_bottom, offset, 0)
    shift_above = jnp.where(at_top, span - offset, 0)
    boost_below = jnp.where(at_bottom, -6.0 * SHEAR_SPEED, 0.0)
    boost_above = jnp.where(at_top, 6.0 * SHEAR_SPEED, 0.0)
    tall = iota((8, 128), 0)

    def propagated(direction):
        c_x, c_y, c_z = VELOCITIES[direction]
        slabs = []
        for x in range(8):
            source = x - c_x
            if c_x == 0 or 0 <= source < 8:
                slab = relaxed[direction, source * 8 : source * 8 + 8, :]
            elif c_x > 0:
                slab = from_left[RIGHTWARD.index(direction)]
            else:
                slab = from_right[LEFTWARD.index(direction)]
            if c_y != 0:
                rows_from, shift, boost = (from_below, shift_below, boost_below) if c_y > 0 else (from_above, shift_above, boost_above)
                slot = (UPWARD if c_y > 0 else DOWNWARD).index(direction)
                place = lax.rem(flow * 8 + (source + span) + shift, span)
                ghost = rows_from[slot, pl.ds(place, 1), :]
                if c_x != 0:
                    ghost = ghost + boost * (WEIGHTS[direction] * c_x)
                slab = pltpu.roll(slab, 1 if c_y > 0 else 7, 0)
                slab = jnp.where(tall == (0 if c_y > 0 else 7), jnp.broadcast_to(ghost, (8, 128)), slab)
            if c_z != 0:
                slab = pltpu.roll(slab, 1 if c_z > 0 else 127, 1)
            slabs.append(slab)
        return jnp.concatenate(slabs, axis=0)

    next_ref[0] = relaxed[0].reshape(8, 8, 128)
    for direction in range(1, 19):
        opposite = direction + 1 if direction % 2 == 1 else direction - 1
        pair, part = (direction - 1) // 2, (direction - 1) % 2
        refs = spread[0, 1 + pair, 8 * part : 8 * part + 8]
        back = bounced[pair, 8 * part : 8 * part + 8]
        next_ref[opposite] = jnp.where(refs >= 0, back, propagated(opposite).reshape(8, 8, 128))

    forces = part_out[4]
    for code in neighbours:
        part_copy(code).wait_recv()
        forces = forces + part_in[code]
    for axis_id in range(3):
        force = forces[axis_id : axis_id + 1, 0:64]
        force_ref[axis_id, 0] = force
        moved_ref[axis_id, 0] = velocity_ref[axis_id, 0] + INV_MASS * force

    for code in neighbours:
        part_copy(code).wait_send()
        speed_copy(code).wait_send()
    for copy in face_copies():
        copy.wait_send()

    def sent_up(step, carry):
        up_copy(column(step), flow).wait_send()
        return carry

    def sent_down(step, carry):
        down_copy(column(step), flow).wait_send()
        return carry

    lax.fori_loop(0, up_targets, sent_up, 0)
    lax.fori_loop(0, down_targets, sent_down, 0)


def hand_over(next_in, force_in, moved_in, next_out, force_out, moved_out, sem):
    copies = [
        pltpu.make_async_copy(force_in, force_out, sem.at[0]),
        pltpu.make_async_copy(moved_in, moved_out, sem.at[1]),
    ]
    for part, (start, end) in enumerate(((0, 5), (5, 10), (10, 15), (15, 19))):
        copies.append(pltpu.make_async_copy(next_in.at[start:end], next_out.at[start:end], sem.at[2 + part]))
    for copy in copies:
        copy.start()
    for copy in copies:
        copy.wait()


def per_device(
    n_flow,
    n_grad,
    populations,
    le_offset,
    sphere_velocity,
    link_cell,
    link_dir,
    link_sphere,
    link_count,
    pair_first,
    pair_second,
    pair_count,
    pair_gap,
    pair_normal,
):
    vmem = pl.BlockSpec(memory_space=pltpu.VMEM)
    hbm = pl.BlockSpec(memory_space=pltpu.HBM)
    smem = pl.BlockSpec(memory_space=pltpu.SMEM)
    span = 8 * n_flow
    f32, i32 = jnp.float32, jnp.int32
    dma = pltpu.SemaphoreType.DMA
    results = pl.pallas_call(
        functools.partial(step_kernel, n_flow, n_grad),
        out_shape=(
            pltpu.VMEM(populations.shape, f32),
            pltpu.VMEM(sphere_velocity.shape, f32),
            pltpu.VMEM(sphere_velocity.shape, f32),
        ),
        in_specs=[smem] * 3 + [hbm] * 9,
        out_specs=(vmem, vmem, vmem),
        scratch_shapes=[
            pltpu.VMEM((19, 8, 8, 128), f32),
            pltpu.VMEM((3, 1, 1, 64), f32),
            pltpu.VMEM((128, 128), i32),
            pltpu.VMEM((128, 128), i32),
            pltpu.VMEM((128, 128), i32),
            pltpu.VMEM((1, 1, 256), i32),
            pltpu.VMEM((1, 1, 256), i32),
            pltpu.VMEM((1, 1, 256), f32),
            pltpu.VMEM((3, 1, 1, 256), f32),
            dma((16,)),
            pltpu.VMEM((19, 64, 128), f32),
            pltpu.VMEM((64, 128), f32),
            pltpu.VMEM((5, 8, 128), f32),
            pltpu.VMEM((5, 8, 128), f32),
            pltpu.VMEM((5, 8, 128), f32),
            pltpu.VMEM((5, 8, 128), f32),
            pltpu.VMEM((5, 8, 128), f32),
            pltpu.VMEM((5, 8, 128), f32),
            pltpu.VMEM((5, span, 128), f32),
            pltpu.VMEM((5, span, 128), f32),
            pltpu.VMEM((8, 128), f32),
            pltpu.VMEM((9, 8, 128), f32),
            pltpu.VMEM((64, 128), f32),
            pltpu.VMEM((128, 128), i32),
            pltpu.VMEM((16, 8, 128), i32),
            pltpu.VMEM((16, 8, 128), i32),
            pltpu.VMEM((15, 10, 16, 8, 128), i32),
            pltpu.VMEM((9, 16, 8, 128), f32),
            pltpu.VMEM((9, 16, 8, 128), f32),
            pltpu.VMEM((7, 8, 8, 128), f32),
            pltpu.VMEM((16, 8, 128), f32),
            pltpu.VMEM((2, 8, 128), i32),
            pltpu.VMEM((4, 8, 128), f32),
            pltpu.VMEM((SUM_ROWS, 128), i32),
            pltpu.VMEM((SUM_ROWS, 128), i32),
            pltpu.VMEM((6, SUM_ROWS, 128), f32),
            pltpu.VMEM((9, 8, 128), f32),
            pltpu.VMEM((9, 8, 128), f32),
            dma((2,)),
            dma((2,)),
            dma((n_flow,)),
            dma((n_flow,)),
            dma((n_flow,)),
            dma((n_flow,)),
            dma((9,)),
            dma((9,)),
            dma((9,)),
            dma((9,)),
        ],
        compiler_params=pltpu.CompilerParams(
            collective_id=0, has_side_effects=True, vmem_limit_bytes=40 * 1024 * 1024
        ),
        name="lattice_step",
    )(
        le_offset,
        link_count,
        pair_count,
        *[
            pltpu.with_memory_space_constraint(operand, pltpu.HBM)
            for operand in (
                populations,
                sphere_velocity,
                link_cell.reshape(128, 128),
                link_dir.reshape(128, 128),
                link_sphere.reshape(128, 128),
                pair_first,
                pair_second,
                pair_gap,
                pair_normal,
            )
        ],
    )
    return pl.pallas_call(
        hand_over,
        out_shape=[jax.ShapeDtypeStruct(result.shape, f32) for result in results],
        in_specs=[vmem] * 3,
        out_specs=[hbm] * 3,
        scratch_shapes=[dma((6,))],
        compiler_params=pltpu.CompilerParams(vmem_limit_bytes=40 * 1024 * 1024),
        name="hand_over",
    )(*results)


def solution(mesh):
    tiled = P(None, "flow", "grad", None)
    listed = P("flow", "grad", None)
    counted = P("flow", "grad")
    return jax.shard_map(
        functools.partial(per_device, mesh.shape["flow"], mesh.shape["grad"]),
        mesh=mesh,
        in_specs=(tiled, P(), tiled, listed, listed, listed, counted, listed, listed, counted, listed, tiled),
        out_specs=(tiled, tiled, tiled),
        check_vma=False,
    )
```

```python
import functools

import jax
import jax.numpy as jnp
from jax import lax
from jax.experimental import pallas as pl
from jax.experimental.pallas import tpu as pltpu
from jax.sharding import PartitionSpec as P

MESH = pl.DeviceIdType.MESH
VELOCITIES = [
    (0, 0, 0),
    (1, 0, 0),
    (-1, 0, 0),
    (0, 1, 0),
    (0, -1, 0),
    (0, 0, 1),
    (0, 0, -1),
    (1, 1, 0),
    (-1, -1, 0),
    (1, -1, 0),
    (-1, 1, 0),
    (1, 0, 1),
    (-1, 0, -1),
    (1, 0, -1),
    (-1, 0, 1),
    (0, 1, 1),
    (0, -1, -1),
    (0, 1, -1),
    (0, -1, 1),
]
WEIGHTS = [1.0 / 3.0] + [1.0 / 18.0] * 6 + [1.0 / 36.0] * 12
UPWARD = [3, 7, 10, 15, 17]
DOWNWARD = [4, 8, 9, 16, 18]
RIGHTWARD = [1, 7, 9, 11, 13]
LEFTWARD = [2, 8, 10, 12, 14]
RELAX_TIME = 0.8
SHEAR_SPEED = 0.1
LUB_COEF = 0.5
GAP_FLOOR = 0.1
GAP_CUTOFF = 1.0
INV_MASS = 1.0 / 523.6

REF_BITS = 10
LANE_UNROLL = 16
ROW_UNROLL = 9
BACK_LANE_UNROLL = 8
BACK_ROW_UNROLL = 9
SUM_UNROLL = 17
DEAD = 1 << 30
LINK_ROWS = 128
SUM_ROWS = LINK_ROWS + 8


def iota(shape, dim):
    return lax.broadcasted_iota(jnp.int32, shape, dim)


def take(table, lanes):
    return jnp.take_along_axis(table, lanes, axis=1, mode="promise_in_bounds")


def collide(current):
    density = current[0]
    for direction in range(1, 19):
        density = density + current[direction]
    inverse = 1.0 / density
    speeds = []
    for axis_id in range(3):
        running = None
        for direction, vector in enumerate(VELOCITIES):
            if vector[axis_id] == 0:
                continue
            value = current[direction]
            if running is None:
                running = value
            elif vector[axis_id] > 0:
                running = running + value
            else:
                running = running - value
        speeds.append(running * inverse)
    speed_sq = speeds[0] * speeds[0] + speeds[1] * speeds[1] + speeds[2] * speeds[2]
    common = 1.0 - 1.5 * speed_sq
    kept = 1.0 - 1.0 / RELAX_TIME
    relaxed = [kept * current[0] + (WEIGHTS[0] / RELAX_TIME) * density * common]
    scaled = {}
    for direction in range(1, 19, 2):
        vector = VELOCITIES[direction]
        weight = WEIGHTS[direction]
        if weight not in scaled:
            scaled[weight] = (weight / RELAX_TIME) * density
        c_dot = None
        for axis_id in range(3):
            if vector[axis_id] != 0:
                term = speeds[axis_id]
                if c_dot is None:
                    c_dot = term
                elif vector[axis_id] > 0:
                    c_dot = c_dot + term
                else:
                    c_dot = c_dot - term
        even = scaled[weight] * (common + 4.5 * c_dot * c_dot)
        odd = scaled[weight] * (3.0 * c_dot)
        relaxed.append(kept * current[direction] + (even + odd))
        relaxed.append(kept * current[direction + 1] + (even - odd))
    return relaxed, density


def bitonic_sort(keys, rows):
    def swap(held, slot):
        rows[slot] = held.reshape(128, 128)
        parts = [rows[slot, pl.ds(64 * half + line, 8, stride=8), :] for half in range(2) for line in range(8)]
        return jnp.stack(parts)

    def exchange(held, bit):
        pairs = held.reshape(8 >> bit, 2, 1 << bit, 8, 128)
        first, second = pairs[:, 0], pairs[:, 1]
        return jnp.stack([jnp.minimum(first, second), jnp.maximum(first, second)], axis=1).reshape(16, 8, 128)

    place = iota((16, 8, 128), 0) + 16 * iota((16, 8, 128), 1) + 128 * iota((16, 8, 128), 2)
    lane = iota((128, 128), 1)
    for phase in range(1, 15):
        flips = place >> (phase - 1)
        if phase == 1:
            flips = place >> 1
        elif phase < 14:
            flips = flips ^ (place >> phase)
        keys = keys ^ (-(flips & 1))
        bit = phase - 1
        while bit >= 7:
            step = 1 << (bit - 7)
            flat = keys.reshape(128, 128)
            partner = take(flat, lane ^ step)
            upper = (lane & step) != 0
            flat = jnp.where(upper, jnp.maximum(flat, partner), jnp.minimum(flat, partner))
            keys = flat.reshape(16, 8, 128)
            bit -= 1
        if bit >= 4:
            keys = swap(keys, phase % 2)
            while bit >= 4:
                keys = exchange(keys, bit - 4)
                bit -= 1
            keys = swap(keys, phase % 2)
        while bit >= 0:
            keys = exchange(keys, bit)
            bit -= 1
    return keys


def step_kernel(
    n_flow,
    n_grad,
    offset_ref,
    link_count_ref,
    pair_count_ref,
    pop_hbm,
    velocity_hbm,
    cell_hbm,
    dir_hbm,
    sphere_hbm,
    first_hbm,
    second_hbm,
    gap_hbm,
    normal_hbm,
    next_ref,
    force_ref,
    moved_ref,
    pop_ref,
    velocity_ref,
    cell_ref,
    dir_ref,
    sphere_ref,
    first_ref,
    second_ref,
    gap_ref,
    normal_ref,
    in_sem,
    relaxed,
    density,
    face_right,
    face_left,
    face_up,
    face_down,
    from_left,
    from_right,
    from_below,
    from_above,
    own_speed,
    near,
    speed_rows,
    sorted_keys,
    sort_rows,
    rests,
    homes,
    spread,
    bounced,
    strength,
    rim,
    pushes,
    pair_ints,
    pair_floats,
    sum_code,
    sum_slot,
    sum_piece,
    part_out,
    part_in,
    face_send,
    face_recv,
    up_send,
    up_recv,
    down_send,
    down_recv,
    speed_send,
    speed_recv,
    part_send,
    part_recv,
):
    flow, grad = lax.axis_index("flow"), lax.axis_index("grad")
    right, left = lax.rem(flow + 1, n_flow), lax.rem(flow + n_flow - 1, n_flow)
    above, below = lax.rem(grad + 1, n_grad), lax.rem(grad + n_grad - 1, n_grad)
    up_targets = jnp.where(grad == n_grad - 1, n_flow, 3)
    down_targets = jnp.where(grad == 0, n_flow, 3)

    def column(step):
        return lax.rem(flow + n_flow - 1 + step, n_flow)

    copies_in = {}

    def bring(name, source, target):
        copies_in[name] = pltpu.make_async_copy(source, target, in_sem.at[len(copies_in)])
        copies_in[name].start()

    bring("velocity", velocity_hbm, velocity_ref)
    for x in range(8):
        bring(x, pop_hbm.at[:, x], pop_ref.at[:, x])
    bring("dir", dir_hbm, dir_ref)
    bring("cell", cell_hbm, cell_ref)
    bring("sphere", sphere_hbm, sphere_ref)
    bring("first", first_hbm, first_ref)
    bring("second", second_hbm, second_ref)
    bring("gap", gap_hbm, gap_ref)
    bring("normal", normal_hbm, normal_ref)

    barrier = pltpu.get_barrier_semaphore()
    for target in (left, right):
        pl.semaphore_signal(barrier, inc=1, device_id=(target, grad), device_id_type=MESH)

    def greet_up(step, carry):
        pl.semaphore_signal(barrier, inc=1, device_id=(column(step), above), device_id_type=MESH)
        return carry

    def greet_down(step, carry):
        pl.semaphore_signal(barrier, inc=1, device_id=(column(step), below), device_id_type=MESH)
        return carry

    lax.fori_loop(0, up_targets, greet_up, 0)
    lax.fori_loop(0, down_targets, greet_down, 0)

    copies_in["velocity"].wait()
    for axis_id in range(3):
        own_speed[axis_id : axis_id + 1, 0:64] = velocity_ref[axis_id, 0]

    def collide_slab(x, carry):
        rows = pl.ds(pl.multiple_of(x * 8, 8), 8)
        values, total = collide([pop_ref[direction, x] for direction in range(19)])
        for direction in range(19):
            relaxed[direction, rows, :] = values[direction]
        density[rows, :] = total
        return carry

    for x in range(8):
        copies_in[x].wait()
    lax.fori_loop(0, 8, collide_slab, 0)
    for slot in range(5):
        face_right[slot] = relaxed[RIGHTWARD[slot], 56:64, :]
        face_left[slot] = relaxed[LEFTWARD[slot], 0:8, :]
        face_up[slot] = relaxed[UPWARD[slot], pl.ds(7, 8, stride=8), :]
        face_down[slot] = relaxed[DOWNWARD[slot], pl.ds(0, 8, stride=8), :]

    def speed_copy(code):
        target = (
            lax.rem(flow + n_flow - (code // 3 - 1), n_flow),
            lax.rem(grad + n_grad - (code % 3 - 1), n_grad),
        )
        return pltpu.make_async_remote_copy(
            src_ref=own_speed,
            dst_ref=near.at[code],
            send_sem=speed_send.at[code],
            recv_sem=speed_recv.at[code],
            device_id=target,
            device_id_type=MESH,
        )

    def part_copy(code):
        target = (
            lax.rem(flow + n_flow + (code // 3 - 1), n_flow),
            lax.rem(grad + n_grad + (code % 3 - 1), n_grad),
        )
        return pltpu.make_async_remote_copy(
            src_ref=part_out.at[code],
            dst_ref=part_in.at[code],
            send_sem=part_send.at[code],
            recv_sem=part_recv.at[code],
            device_id=target,
            device_id_type=MESH,
        )

    neighbours = [0, 2, 6, 8, 1, 7, 3, 5]

    def face_copies():
        return (
            pltpu.make_async_remote_copy(
                src_ref=face_right,
                dst_ref=from_left,
                send_sem=face_send.at[0],
                recv_sem=face_recv.at[0],
                device_id=(right, grad),
                device_id_type=MESH,
            ),
            pltpu.make_async_remote_copy(
                src_ref=face_left,
                dst_ref=from_right,
                send_sem=face_send.at[1],
                recv_sem=face_recv.at[1],
                device_id=(left, grad),
                device_id_type=MESH,
            ),
        )

    def up_copy(target, source):
        return pltpu.make_async_remote_copy(
            src_ref=face_up,
            dst_ref=from_below.at[:, pl.ds(pl.multiple_of(source * 8, 8), 8), :],
            send_sem=up_send.at[target],
            recv_sem=up_recv.at[source],
            device_id=(target, above),
            device_id_type=MESH,
        )

    def down_copy(target, source):
        return pltpu.make_async_remote_copy(
            src_ref=face_down,
            dst_ref=from_above.at[:, pl.ds(pl.multiple_of(source * 8, 8), 8), :],
            send_sem=down_send.at[target],
            recv_sem=down_recv.at[source],
            device_id=(target, below),
            device_id_type=MESH,
        )

    def send_up(step, carry):
        up_copy(column(step), flow).start()
        return carry

    def send_down(step, carry):
        down_copy(column(step), flow).start()
        return carry

    def send_all():
        pl.semaphore_wait(barrier, 2 + up_targets + down_targets)
        for code in neighbours:
            speed_copy(code).start()
        for copy in face_copies():
            copy.start()
        lax.fori_loop(0, up_targets, send_up, 0)
        lax.fori_loop(0, down_targets, send_down, 0)

    sends_later = jnp.logical_and(jnp.logical_or(grad == 0, grad == n_grad - 1), flow < n_flow // 2)
    pl.when(jnp.logical_not(sends_later))(send_all)

    copies_in["dir"].wait()
    copies_in["cell"].wait()
    copies_in["sphere"].wait()
    kinds, cells = dir_ref[...] - 1, cell_ref[...]
    packed = ((kinds >> 1) << 24) | ((cells & 127) << 17) | ((kinds & 1) << 16) | ((cells >> 7) << REF_BITS) | sphere_ref[...]
    listed = iota((128, 128), 0) * 128 + iota((128, 128), 1)
    packed = jnp.where(listed < link_count_ref[0, 0], packed, DEAD)
    ordered = bitonic_sort(packed.reshape(16, 8, 128), sort_rows)
    sorted_keys[...] = ordered.reshape(128, 128)
    picked = [sorted_keys[pl.ds(sublane, 16, stride=8), :] for sublane in range(8)]
    natural = jnp.concatenate(picked, axis=0)
    sorted_keys[...] = natural
    number = iota((128, 128), 1) * 128 + iota((128, 128), 0)
    lag = natural - (number << REF_BITS)
    rests[...] = (lag & ((1 << 24) - 1)).reshape(16, 8, 128)
    homes[...] = (lag >> 24).reshape(16, 8, 128)
    for level in range(1, 8):
        spread[level, 0] = jnp.full((16, 8, 128), -1, jnp.int32)

    def advance(held, coming, unit):
        return jnp.where(coming >= unit, coming - unit, jnp.where(held < unit, held, -1))

    def spread_lanes(line, carry):
        rest, home = rests[line], homes[line]
        lane = iota((9, 8, 128), 2)
        edge = jnp.full((1, 8, 128), -1, jnp.int32)
        held = jnp.stack([jnp.where(home == block, rest, -1) for block in range(9)])
        for bit in range(13, 6, -1):
            spread[bit + 1, 1:10, line] = held
            step = 1 << (bit - 7)
            before = jnp.concatenate([edge, held[:8]], axis=0)
            coming = pltpu.roll(jnp.where(lane >= 128 - step, before, held), step, 2)
            held = advance(held, coming, 1 << (bit + REF_BITS))
        spread[7, 1:10, line] = held
        return carry

    lax.fori_loop(0, 16, spread_lanes, 0, unroll=LANE_UNROLL)

    def spread_rows(block, carry):
        sublane = iota((16, 8, 128), 1)
        held = spread[7, block + 1]
        for bit in range(6, -1, -1):
            if bit < 6:
                spread[bit + 1, block + 1] = held
            count = max(1 << bit, 8) // 8
            last = iota((count, 8, 128), 2) == 127
            around = jnp.where(last, spread[bit + 1, block, 16 - count : 16], held[16 - count :])
            before = jnp.concatenate([pltpu.roll(around, 1, 2), held[: 16 - count]], axis=0)
            if bit < 3:
                step = 1 << bit
                before = pltpu.roll(jnp.where(sublane >= 8 - step, before, held), step, 1)
            held = advance(held, before, 1 << (bit + REF_BITS))
        spread[0, block + 1] = held
        return carry

    lax.fori_loop(0, 9, spread_rows, 0, unroll=ROW_UNROLL)

    pl.when(sends_later)(send_all)

    for code in neighbours:
        speed_copy(code).wait_recv()
    near[4] = own_speed[...]
    half = iota((8, 128), 1) < 64
    for pair in range(5):
        row = near[2 * pair]
        if pair < 4:
            row = jnp.where(half, row, pltpu.roll(near[2 * pair + 1], 64, 1))
        for axis_id in range(3):
            speed_rows[45 + 5 * axis_id + pair : 46 + 5 * axis_id + pair, :] = row[axis_id : axis_id + 1]
        for line in range(9):
            vector = VELOCITIES[2 * line + 1]
            total = None
            for axis_id in range(3):
                if vector[axis_id] != 0:
                    term = row[axis_id : axis_id + 1]
                    if total is None:
                        total = term
                    elif vector[axis_id] > 0:
                        total = total + term
                    else:
                        total = total - term
            speed_rows[5 * line + pair : 5 * line + pair + 1, :] = total

    def speed_of(line, refs):
        lanes = refs & 127
        group = refs >> 7
        found = take(jnp.broadcast_to(speed_rows[5 * line : 5 * line + 1, :], refs.shape), lanes)
        for pair in range(1, 5):
            row = jnp.broadcast_to(speed_rows[5 * line + pair : 5 * line + pair + 1, :], refs.shape)
            found = jnp.where(group == pair, take(row, lanes), found)
        return found

    for direction in range(1, 19):
        sign = 1.0 if direction % 2 == 1 else -1.0
        pair, part = (direction - 1) // 2, (direction - 1) % 2
        refs = spread[0, 1 + pair, 8 * part : 8 * part + 8].reshape(64, 128)
        leaving = relaxed[direction]
        back = leaving - (6.0 * WEIGHTS[direction] * sign) * density[...] * speed_of(pair, refs)
        bounced[pair, 8 * part : 8 * part + 8] = back.reshape(8, 8, 128)
        strength[pair, 8 * part : 8 * part + 8] = (leaving + back).reshape(8, 8, 128)

    def gather_rows(turn, carry):
        block = 8 - turn
        sublane = iota((16, 8, 128), 1)
        held = strength[block]
        for bit in range(7):
            count = max(1 << bit, 8) // 8
            first = iota((count, 8, 128), 2) == 0
            around = jnp.where(first, rim[bit, 0:count], held[:count])
            rim[bit, 0:count] = held[:count]
            after = jnp.concatenate([held[count:], pltpu.roll(around, 127, 2)], axis=0)
            if bit < 3:
                step = 1 << bit
                after = pltpu.roll(jnp.where(sublane < step, after, held), 8 - step, 1)
            held = jnp.where(spread[bit + 1, block + 1] >= 1 << (bit + REF_BITS), after, held)
        strength[block] = held
        return carry

    lax.fori_loop(0, 9, gather_rows, 0, unroll=BACK_ROW_UNROLL)

    def gather_lanes(line, carry):
        lane = iota((9, 8, 128), 2)
        held = strength[:, line]
        for bit in range(7, 14):
            step = 1 << (bit - 7)
            after = jnp.concatenate([held[1:], held[8:]], axis=0)
            ahead = pltpu.roll(jnp.where(lane < step, after, held), 128 - step, 2)
            held = jnp.where(spread[bit + 1, 1:10, line] >= 1 << (bit + REF_BITS), ahead, held)
        home = homes[line]
        push = jnp.zeros((8, 128), jnp.float32)
        for block in range(9):
            push = jnp.where(home == block, held[block], push)
        pushes[line] = push
        return carry

    lax.fori_loop(0, 16, gather_lanes, 0, unroll=BACK_LANE_UNROLL)
    keys = sorted_keys[...]
    push = pushes[...].reshape(128, 128)

    def put_terms(rows, refs, terms):
        sum_code[rows, :] = refs >> 6
        sum_slot[rows, :] = refs & 63
        for axis_id in range(3):
            coarse = terms[axis_id].astype(jnp.bfloat16).astype(jnp.float32)
            sum_piece[axis_id, rows, :] = coarse
            sum_piece[3 + axis_id, rows, :] = terms[axis_id] - coarse

    kind = (((keys >> 24) << 1) | ((keys >> 16) & 1)) & 127
    small_lane = iota((8, 128), 1)
    terms = []
    for axis_id in range(3):
        table = jnp.zeros((8, 128), jnp.float32)
        for direction in range(1, 19):
            part = VELOCITIES[direction][axis_id]
            if part != 0:
                table = jnp.where(small_lane == direction - 1, float(part), table)
        tall_table = jnp.concatenate([table] * 16, axis=0)
        terms.append(take(tall_table, kind) * push)
    put_terms(pl.ds(0, 128), keys & 1023, terms)

    for name in ("first", "second", "gap", "normal"):
        copies_in[name].wait()
    pair_ints[...] = jnp.zeros((2, 8, 128), jnp.int32)
    pair_floats[...] = jnp.ones((4, 8, 128), jnp.float32)
    for row in range(2):
        lanes = slice(row * 128, row * 128 + 128)
        pair_ints[0, row : row + 1, :] = first_ref[0, :, lanes] + 256
        pair_ints[1, row : row + 1, :] = second_ref[0, :, lanes]
        pair_floats[3, row : row + 1, :] = gap_ref[0, :, lanes]
        for axis_id in range(3):
            pair_floats[axis_id, row : row + 1, :] = normal_ref[axis_id, 0, :, lanes]
    heads, tails = pair_ints[0], pair_ints[1]
    normals = [pair_floats[axis_id] for axis_id in range(3)]
    rate = None
    for axis_id in range(3):
        gap_speed = (speed_of(9 + axis_id, heads) - speed_of(9 + axis_id, tails)) * normals[axis_id]
        rate = gap_speed if rate is None else rate + gap_speed
    resist = LUB_COEF * (1.0 / jnp.maximum(pair_floats[3], GAP_FLOOR) - 1.0 / GAP_CUTOFF)
    alive = iota((8, 128), 0) * 128 + small_lane < jnp.minimum(pair_count_ref[0, 0], 256)
    scale = jnp.where(alive, -resist * rate, 0.0)
    lift = [scale * normals[axis_id] for axis_id in range(3)]
    lower = iota((8, 128), 0) < 2
    both = jnp.where(lower, heads, pltpu.roll(tails, 2, 0))
    lift = [jnp.where(lower, term, -pltpu.roll(term, 2, 0)) for term in lift]
    put_terms(pl.ds(128, 8), both, lift)

    code_rows = iota((16, 128), 0)
    slot_rows = iota((64, 128), 0)

    def add_rows(group, total):
        base = group * 8
        pieces, slots = [], []
        for row in range(8):
            at = pl.ds(base + row, 1)
            chosen = code_rows == jnp.broadcast_to(sum_code[at, :], (16, 128))
            parts = [
                jnp.where(chosen, jnp.broadcast_to(sum_piece[piece, at, :], (16, 128)), 0.0).astype(jnp.bfloat16)
                for piece in range(6)
            ]
            pieces.append(jnp.concatenate(parts, axis=0))
            slot = slot_rows == jnp.broadcast_to(sum_slot[at, :], (64, 128))
            slots.append(jnp.where(slot, 1.0, 0.0).astype(jnp.bfloat16))
        return total + lax.dot_general(
            jnp.concatenate(pieces, axis=1),
            jnp.concatenate(slots, axis=1),
            (((1,), (1,)), ((), ())),
            preferred_element_type=jnp.float32,
        )

    total = lax.fori_loop(0, SUM_ROWS // 8, add_rows, jnp.zeros((96, 64), jnp.float32), unroll=SUM_UNROLL)
    for axis_id in range(3):
        summed = total[16 * axis_id : 16 * axis_id + 16] + total[48 + 16 * axis_id : 64 + 16 * axis_id]
        for code in range(9):
            part_out[code, axis_id : axis_id + 1, 0:64] = summed[code : code + 1]

    for code in neighbours:
        part_copy(code).start()
    def came_up(step, carry):
        up_copy(column(step), column(step)).wait_recv()
        return carry

    def came_down(step, carry):
        down_copy(column(step), column(step)).wait_recv()
        return carry

    lax.fori_loop(0, down_targets, came_up, 0)
    lax.fori_loop(0, up_targets, came_down, 0)
    for copy in face_copies():
        copy.wait_recv()

    span = 8 * n_flow
    offset = offset_ref[0]
    at_bottom, at_top = grad == 0, grad == n_grad - 1
    shift_below = jnp.where(at_bottom, offset, 0)
    shift_above = jnp.where(at_top, span - offset, 0)
    boost_below = jnp.where(at_bottom, -6.0 * SHEAR_SPEED, 0.0)
    boost_above = jnp.where(at_top, 6.0 * SHEAR_SPEED, 0.0)
    tall = iota((8, 128), 0)

    def propagated(direction):
        c_x, c_y, c_z = VELOCITIES[direction]
        slabs = []
        for x in range(8):
            source = x - c_x
            if c_x == 0 or 0 <= source < 8:
                slab = relaxed[direction, source * 8 : source * 8 + 8, :]
            elif c_x > 0:
                slab = from_left[RIGHTWARD.index(direction)]
            else:
                slab = from_right[LEFTWARD.index(direction)]
            if c_y != 0:
                rows_from, shift, boost = (from_below, shift_below, boost_below) if c_y > 0 else (from_above, shift_above, boost_above)
                slot = (UPWARD if c_y > 0 else DOWNWARD).index(direction)
                place = lax.rem(flow * 8 + (source + span) + shift, span)
                ghost = rows_from[slot, pl.ds(place, 1), :]
                if c_x != 0:
                    ghost = ghost + boost * (WEIGHTS[direction] * c_x)
                slab = pltpu.roll(slab, 1 if c_y > 0 else 7, 0)
                slab = jnp.where(tall == (0 if c_y > 0 else 7), jnp.broadcast_to(ghost, (8, 128)), slab)
            if c_z != 0:
                slab = pltpu.roll(slab, 1 if c_z > 0 else 127, 1)
            slabs.append(slab)
        return jnp.concatenate(slabs, axis=0)

    next_ref[0] = relaxed[0].reshape(8, 8, 128)
    for direction in range(1, 19):
        opposite = direction + 1 if direction % 2 == 1 else direction - 1
        pair, part = (direction - 1) // 2, (direction - 1) % 2
        refs = spread[0, 1 + pair, 8 * part : 8 * part + 8]
        back = bounced[pair, 8 * part : 8 * part + 8]
        next_ref[opposite] = jnp.where(refs >= 0, back, propagated(opposite).reshape(8, 8, 128))

    for code in neighbours:
        speed_copy(code).wait_send()
    for copy in face_copies():
        copy.wait_send()

    def sent_up(step, carry):
        up_copy(column(step), flow).wait_send()
        return carry

    def sent_down(step, carry):
        down_copy(column(step), flow).wait_send()
        return carry

    lax.fori_loop(0, up_targets, sent_up, 0)
    lax.fori_loop(0, down_targets, sent_down, 0)

    forces = part_out[4]
    for code in neighbours:
        part_copy(code).wait_recv()
        forces = forces + part_in[code]
    for axis_id in range(3):
        force = forces[axis_id : axis_id + 1, 0:64]
        force_ref[axis_id, 0] = force
        moved_ref[axis_id, 0] = velocity_ref[axis_id, 0] + INV_MASS * force

    for code in neighbours:
        part_copy(code).wait_send()


def hand_over(next_in, force_in, moved_in, next_out, force_out, moved_out, sem):
    copies = [
        pltpu.make_async_copy(force_in, force_out, sem.at[0]),
        pltpu.make_async_copy(moved_in, moved_out, sem.at[1]),
    ]
    for part, (start, end) in enumerate(((0, 5), (5, 10), (10, 15), (15, 19))):
        copies.append(pltpu.make_async_copy(next_in.at[start:end], next_out.at[start:end], sem.at[2 + part]))
    for copy in copies:
        copy.start()
    for copy in copies:
        copy.wait()


def per_device(
    n_flow,
    n_grad,
    populations,
    le_offset,
    sphere_velocity,
    link_cell,
    link_dir,
    link_sphere,
    link_count,
    pair_first,
    pair_second,
    pair_count,
    pair_gap,
    pair_normal,
):
    vmem = pl.BlockSpec(memory_space=pltpu.VMEM)
    hbm = pl.BlockSpec(memory_space=pltpu.HBM)
    smem = pl.BlockSpec(memory_space=pltpu.SMEM)
    span = 8 * n_flow
    f32, i32 = jnp.float32, jnp.int32
    dma = pltpu.SemaphoreType.DMA
    results = pl.pallas_call(
        functools.partial(step_kernel, n_flow, n_grad),
        out_shape=(
            pltpu.VMEM(populations.shape, f32),
            pltpu.VMEM(sphere_velocity.shape, f32),
            pltpu.VMEM(sphere_velocity.shape, f32),
        ),
        in_specs=[smem] * 3 + [hbm] * 9,
        out_specs=(vmem, vmem, vmem),
        scratch_shapes=[
            pltpu.VMEM((19, 8, 8, 128), f32),
            pltpu.VMEM((3, 1, 1, 64), f32),
            pltpu.VMEM((128, 128), i32),
            pltpu.VMEM((128, 128), i32),
            pltpu.VMEM((128, 128), i32),
            pltpu.VMEM((1, 1, 256), i32),
            pltpu.VMEM((1, 1, 256), i32),
            pltpu.VMEM((1, 1, 256), f32),
            pltpu.VMEM((3, 1, 1, 256), f32),
            dma((16,)),
            pltpu.VMEM((19, 64, 128), f32),
            pltpu.VMEM((64, 128), f32),
            pltpu.VMEM((5, 8, 128), f32),
            pltpu.VMEM((5, 8, 128), f32),
            pltpu.VMEM((5, 8, 128), f32),
            pltpu.VMEM((5, 8, 128), f32),
            pltpu.VMEM((5, 8, 128), f32),
            pltpu.VMEM((5, 8, 128), f32),
            pltpu.VMEM((5, span, 128), f32),
            pltpu.VMEM((5, span, 128), f32),
            pltpu.VMEM((8, 128), f32),
            pltpu.VMEM((9, 8, 128), f32),
            pltpu.VMEM((64, 128), f32),
            pltpu.VMEM((128, 128), i32),
            pltpu.VMEM((2, 128, 128), i32),
            pltpu.VMEM((16, 8, 128), i32),
            pltpu.VMEM((16, 8, 128), i32),
            pltpu.VMEM((15, 10, 16, 8, 128), i32),
            pltpu.VMEM((9, 16, 8, 128), f32),
            pltpu.VMEM((9, 16, 8, 128), f32),
            pltpu.VMEM((7, 8, 8, 128), f32),
            pltpu.VMEM((16, 8, 128), f32),
            pltpu.VMEM((2, 8, 128), i32),
            pltpu.VMEM((4, 8, 128), f32),
            pltpu.VMEM((SUM_ROWS, 128), i32),
            pltpu.VMEM((SUM_ROWS, 128), i32),
            pltpu.VMEM((6, SUM_ROWS, 128), f32),
            pltpu.VMEM((9, 8, 128), f32),
            pltpu.VMEM((9, 8, 128), f32),
            dma((2,)),
            dma((2,)),
            dma((n_flow,)),
            dma((n_flow,)),
            dma((n_flow,)),
            dma((n_flow,)),
            dma((9,)),
            dma((9,)),
            dma((9,)),
            dma((9,)),
        ],
        compiler_params=pltpu.CompilerParams(
            collective_id=0, has_side_effects=True, vmem_limit_bytes=40 * 1024 * 1024
        ),
        name="lattice_step",
    )(
        le_offset,
        link_count,
        pair_count,
        *[
            pltpu.with_memory_space_constraint(operand, pltpu.HBM)
            for operand in (
                populations,
                sphere_velocity,
                link_cell.reshape(128, 128),
                link_dir.reshape(128, 128),
                link_sphere.reshape(128, 128),
                pair_first,
                pair_second,
                pair_gap,
                pair_normal,
            )
        ],
    )
    return pl.pallas_call(
        hand_over,
        out_shape=[jax.ShapeDtypeStruct(result.shape, f32) for result in results],
        in_specs=[vmem] * 3,
        out_specs=[hbm] * 3,
        scratch_shapes=[dma((6,))],
        compiler_params=pltpu.CompilerParams(vmem_limit_bytes=40 * 1024 * 1024),
        name="hand_over",
    )(*results)


def solution(mesh):
    tiled = P(None, "flow", "grad", None)
    listed = P("flow", "grad", None)
    counted = P("flow", "grad")
    return jax.shard_map(
        functools.partial(per_device, mesh.shape["flow"], mesh.shape["grad"]),
        mesh=mesh,
        in_specs=(tiled, P(), tiled, listed, listed, listed, counted, listed, listed, counted, listed, tiled),
        out_specs=(tiled, tiled, tiled),
        check_vma=False,
    )
```
